512 devices in a mesh: row: 8 (over z), col: 64 (over x, y, core).
Axes of the slice: x: 4, y: 8, z: 8, core: 2. Of those that a mesh axis runs over, the one named last changes fastest.
Arguments:
- top_multipoles: bfloat16 [2048, 256], P('row'), may hold values from -6 to 6
- coarse_multipoles: bfloat16 [16384, 256], P(('row', 'col')), may hold values from -6 to 6
- fine_multipoles: bfloat16 [131072, 256], P(('row', 'col')), may hold values from -6 to 6
- m2l_ops: bfloat16 [16, 256, 256], replicated, may hold values from -0.09375 to 0.09375
- l2l_ops: bfloat16 [8, 256, 256], replicated, may hold values from -0.375 to 0.375
- top_source: int32 [512, 16, 24], P(('row', 'col')), may hold values from 0 to 2047, as said below
- top_target: int32 [512, 16, 24], P(('row', 'col')), may hold values from 0 to 256, as said below
- coarse_source: int32 [512, 16, 96], P(('row', 'col')), may hold values from 0 to 16383, as said below
- coarse_target: int32 [512, 16, 96], P(('row', 'col')), may hold values from 0 to 32, as said below
- fine_source: int32 [512, 16, 384], P(('row', 'col')), may hold values from 0 to 767, as said below
- fine_target: int32 [512, 16, 384], P(('row', 'col')), may hold values from 0 to 256, as said below
Outputs:
- fine_local: float32 [131072, 256], P(('row', 'col'))
The draws below stay inside these ranges and needn't reach their ends.
Inputs may be any that keep to these rules, and one draw needn't show every extreme that they name: `top_source`: A slot of device d in coarse segment g = d // 64 names a source in [(g - 1) * 256, (g + 2) * 256). `top_target`: the value 256 marks an empty slot. `coarse_source`: A slot of device d names a source in [(d - 1) * 32, (d + 2) * 32). `coarse_target`: the value 32 marks an empty slot. A slot of device d names the finest-level box (d - 1) * 256 + fine_source, which lies in [0, 131072). `fine_target`: the value 256 marks an empty slot.
All inputs are finite; a program needn't handle non-finite values.
Results may differ from the reference program's by a relative error of at most 0.0034.
Values may be sent and summed in bfloat16 or wider, within the bound.
A program may use at most 64 MiB of HBM per device.

```python
import jax
import jax.numpy as jnp
from jax import lax

COEFFS = 256
R = 16
B = 256
CAP = 384
CAPC = 96
CAPT = 24
NB = 131072
CB = 32
NC = 16384
TG = 256
NT = 2048
N_ROW = 8
N_COL = 64
DEVICES = 512


def source_list(key, per, blocks, group_size, cap):
    block = (jnp.arange(DEVICES, dtype=jnp.int32) // group_size)[:, None, None]
    offset = jax.random.randint(key, (DEVICES, R, cap), -per, 2 * per)
    return jnp.clip(block * per + offset, 0, blocks * per - 1).astype(jnp.int32)


def relative_list(key, per, cap):
    device = jnp.arange(DEVICES, dtype=jnp.int32)[:, None, None]
    offset = jax.random.randint(key, (DEVICES, R, cap), 0, 3 * per)
    lower = jnp.where(device == 0, per, 0)
    upper = jnp.where(device == DEVICES - 1, 2 * per - 1, 3 * per - 1)
    chosen = jnp.clip(offset, lower, upper).astype(jnp.int32)
    chosen = chosen.at[1, 0, 0].set(3 * per - 1)
    chosen = chosen.at[1, 0, 1].set(0)
    return chosen.astype(jnp.int32)


def target_list(key, count, cap):
    first, second = jax.random.split(key)
    target = jax.random.randint(first, (DEVICES, R, cap), 0, count)
    live = jax.random.randint(second, (DEVICES, R, cap), 0, 5) < 3
    return jnp.where(live, target, count).astype(jnp.int32)


def draw_top_source(key, part):
    key = jax.random.fold_in(key, 11)
    return source_list(key, TG, N_ROW, N_COL, CAPT)


def draw_top_target(key, part):
    key = jax.random.fold_in(key, 12)
    return target_list(key, TG, CAPT)


def draw_coarse_source(key, part):
    key = jax.random.fold_in(key, 13)
    return source_list(key, CB, DEVICES, 1, CAPC)


def draw_coarse_target(key, part):
    key = jax.random.fold_in(key, 14)
    return target_list(key, CB, CAPC)


def draw_fine_source(key, part):
    key = jax.random.fold_in(key, 15)
    return relative_list(key, B, CAP)


def draw_fine_target(key, part):
    key = jax.random.fold_in(key, 16)
    return target_list(key, B, CAP)


def block_scale(rng, extent, cuts, low, top_value):
    def one(position, shards_of):
        draws = jax.random.uniform(jax.random.fold_in(jax.random.fold_in(rng, 6), position), (shards_of,), jnp.float32, low / len(cuts), top_value / len(cuts))
        return jnp.repeat(jnp.exp(draws), extent[position] // shards_of).reshape((-1,) + (1,) * (len(extent) - position - 1))

    level = one(*cuts[0])
    for cut in cuts[1:]:
        level = level * one(*cut)
    return level


def noise(own_key, dims, scale, most, pieces=(), kind=jnp.bfloat16):
    entries = scale * jax.random.normal(own_key, dims, jnp.float32)
    if pieces:
        entries = entries * block_scale(own_key, dims, pieces, -0.22, 0.18)
    return jnp.clip(entries, -most, most).astype(kind)


def setup_inputs(seed: int = 0) -> dict:
    key_of = jax.random.split(jax.random.key(seed), 12)
    return {
        "top_multipoles": noise(key_of[0], (NT, COEFFS), 1.0, 6.0, ((0, 8),)),
        "coarse_multipoles": noise(key_of[1], (NC, COEFFS), 1.0, 6.0, ((0, 512),)),
        "fine_multipoles": noise(key_of[2], (NB, COEFFS), 1.0, 6.0, ((0, 512),)),
        "m2l_ops": noise(key_of[3], (R, COEFFS, COEFFS), (16 * COEFFS) ** -0.5, 0.09375),
        "l2l_ops": noise(key_of[4], (8, COEFFS, COEFFS), COEFFS ** -0.5, 0.375),
        "top_source": draw_top_source(jax.random.fold_in(key_of[11], 71), 0),
        "top_target": draw_top_target(jax.random.fold_in(key_of[11], 71), 0),
        "coarse_source": draw_coarse_source(jax.random.fold_in(key_of[11], 71), 0),
        "coarse_target": draw_coarse_target(jax.random.fold_in(key_of[11], 71), 0),
        "fine_source": draw_fine_source(jax.random.fold_in(key_of[11], 71), 0),
        "fine_target": draw_fine_target(jax.random.fold_in(key_of[11], 71), 0),
    }


def spread(sources, src, tgt, ops, count):
    def turn(r, acc):
        rows = jnp.take(sources, src[:, r, :].reshape(-1), axis=0)
        prod = jnp.dot(rows, ops[r], preferred_element_type=jnp.float32)
        return acc.at[tgt[:, r, :].reshape(-1)].add(prod)
    start = jnp.zeros((count + 1, sources.shape[1]), jnp.float32)
    acc = lax.fori_loop(0, ops.shape[0], turn, start)
    return acc[:count]


def descend(parents, l2l_ops):
    child = jnp.einsum('pd,ode->poe', parents.astype(jnp.float32), l2l_ops.astype(jnp.float32))
    return child.reshape(-1, parents.shape[1])


def reference(top_multipoles, coarse_multipoles, fine_multipoles, m2l_ops, l2l_ops, top_source, top_target, coarse_source, coarse_target, fine_source, fine_target):
    device = jnp.arange(DEVICES, dtype=jnp.int32)[:, None, None]
    group = device // N_COL
    top_glob = jnp.where(top_target == TG, NT, group * TG + top_target).astype(jnp.int32)
    top_local = spread(top_multipoles, top_source, top_glob, m2l_ops, NT).astype(jnp.bfloat16)
    coarse_glob = jnp.where(coarse_target == CB, NC, device * CB + coarse_target).astype(jnp.int32)
    coarse_sum = descend(top_local, l2l_ops) + spread(coarse_multipoles, coarse_source, coarse_glob, m2l_ops, NC)
    coarse_local = coarse_sum.astype(jnp.bfloat16)
    fine_glob = jnp.where(fine_target == B, NB, device * B + fine_target).astype(jnp.int32)
    fine_from = ((device - 1) * B + fine_source).astype(jnp.int32)
    return descend(coarse_local, l2l_ops) + spread(fine_multipoles, fine_from, fine_glob, m2l_ops, NB)
```

```python
import functools

import jax
import jax.numpy as jnp
from jax import lax
from jax.experimental import pallas as pl
from jax.experimental.pallas import tpu as pltpu
from jax.sharding import PartitionSpec as P

CORES = 2
XS = 4
MESH = pl.DeviceIdType.MESH
BF = jnp.bfloat16
F32 = jnp.float32


def onehot(rows, picks):
    number = lax.broadcasted_iota(jnp.int32, (rows, picks.shape[1]), 0)
    return jnp.where(number == picks, 1.0, 0.0).astype(BF)


def dot(a, b):
    return jnp.dot(a, b, preferred_element_type=F32)


def dot_nt(a, b):
    return lax.dot_general(a, b, (((1,), (1,)), ((), ())), preferred_element_type=F32)


def split(a):
    hi = a.astype(BF)
    return hi, (a - hi.astype(F32)).astype(BF)


def children(parents, ops):
    n, c = parents.shape
    octants, depth, _ = ops.shape
    rep = jnp.broadcast_to(parents[:, None, :], (n, octants, c)).reshape(n * octants, c)
    which = lax.broadcasted_iota(jnp.int32, (n, octants, c), 1).reshape(n * octants, c)
    parts = [jnp.where(which == o, rep, 0.0).astype(BF) for o in range(octants)]
    return dot(jnp.concatenate(parts, axis=1), ops.reshape(octants * depth, c))


def kernel(
    n_row,
    n_col,
    top_ref,
    coarse_ref,
    fine_ref,
    m2l_ref,
    l2l_ref,
    tsrc_ref,
    ttgt_ref,
    csrc_ref,
    ctgt_ref,
    fsrc_ref,
    ftgt_ref,
    out_ref,
    twin,
    cwin,
    fwin,
    ops,
    l2l,
    tsrc,
    ttgt,
    csrc,
    ctgt,
    fsrc,
    ftgt,
    square,
    mine,
    lists,
    tpick,
    cpick,
    ctop,
    ccoarse,
    cfine,
    atop,
    acoarse,
    acc,
    outbox,
    inbox,
    local_sem,
    wsend,
    wrecv,
    lsend,
    lrecv,
    rsend,
    rrecv,
):
    classes, coeffs = m2l_ref.shape[0], m2l_ref.shape[1]
    seg = top_ref.shape[0]
    half = seg // CORES
    quarter = seg // XS
    cb, b = coarse_ref.shape[0], fine_ref.shape[0]
    capt = tsrc_ref.shape[2]
    capc = csrc_ref.shape[2]
    ys = n_col // (XS * CORES)
    mates = XS * CORES
    planes = ys * CORES

    row, col = lax.axis_index("row"), lax.axis_index("col")
    x, j = col // planes, lax.rem(col, planes)
    y, core = j // CORES, lax.rem(col, CORES)
    device = row * n_col + col
    total = n_row * n_col

    def place(index):
        return (index // n_col, lax.rem(index, n_col))

    after = place(lax.rem(device + 1, total))
    before = place(lax.rem(device + total - 1, total))
    above = (lax.rem(row + 1, n_row), col)
    below = (lax.rem(row + n_row - 1, n_row), col)

    def mate(k):
        m = lax.rem(x * CORES + core + k, mates)
        return (row, (m // CORES) * planes + y * CORES + lax.rem(m, CORES))

    def peer(k):
        return (row, x * planes + lax.rem(j + k, planes))

    barrier = pltpu.get_barrier_semaphore()
    partners = [after, before, above, below]
    partners += [mate(k) for k in range(1, mates)]
    partners += [peer(k) for k in range(1, planes)]
    for partner in partners:
        pl.semaphore_signal(barrier, inc=1, device_id=partner, device_id_type=MESH)

    own_top = top_ref.at[pl.ds(pl.multiple_of(core * half, half), half)]
    moves = [
        (tsrc_ref, tsrc),
        (ttgt_ref, ttgt),
        (fsrc_ref, fsrc),
        (ftgt_ref, ftgt),
        (csrc_ref, csrc),
        (ctgt_ref, ctgt),
        (own_top, twin.at[pl.ds(half, half)]),
        (coarse_ref, cwin.at[pl.ds(cb, cb)]),
        (m2l_ref, ops),
        (fine_ref, fwin.at[pl.ds(b, b)]),
        (l2l_ref, l2l),
    ]
    moves = [pltpu.make_async_copy(s, d, local_sem.at[i]) for i, (s, d) in enumerate(moves)]
    for move in moves:
        move.start()

    square[...] = jnp.zeros_like(square)
    unused = lists.shape[0] - mates * capt
    lists[pl.ds(mates * capt, unused)] = jnp.full((unused, lists.shape[1]), -1, jnp.int32)
    moves[0].wait()
    moves[1].wait()
    square[pl.ds(0, classes), pl.ds(0, capt)] = tsrc[0]
    square[pl.ds(classes, classes), pl.ds(0, capt)] = ttgt[0]
    columns = square[...].T[:capt]
    mine[...] = columns
    lists[pl.ds(0, capt)] = columns

    pl.semaphore_wait(barrier, len(partners))

    def remote(src, dst, send, recv, to):
        return pltpu.make_async_remote_copy(
            src_ref=src, dst_ref=dst, send_sem=send, recv_sem=recv, device_id=to, device_id_type=MESH
        )

    windows = [
        (own_top, twin.at[pl.ds(0, half)], above),
        (own_top, twin.at[pl.ds(2 * half, half)], below),
        (coarse_ref, cwin.at[pl.ds(0, cb)], after),
        (coarse_ref, cwin.at[pl.ds(2 * cb, cb)], before),
        (fine_ref, fwin.at[pl.ds(0, b)], after),
        (fine_ref, fwin.at[pl.ds(2 * b, b)], before),
    ]
    windows = [remote(s, d, wsend.at[i], wrecv.at[i], to) for i, (s, d, to) in enumerate(windows)]
    posts = [
        remote(mine, lists.at[pl.ds(k * capt, capt)], lsend.at[k], lrecv.at[k], mate(k))
        for k in range(1, mates)
    ]
    for copy in windows[:2] + posts + windows[2:]:
        copy.start()

    for i in (2, 3, 4, 5):
        moves[i].wait()

    def fine_counts(r, _):
        targets = onehot(b, ftgt[0, pl.ds(r, 1), :])
        sources = onehot(3 * b, fsrc[0, pl.ds(r, 1), :])
        cfine[r] = dot_nt(targets, sources).astype(BF)
        return 0

    cpick[...] = jnp.full(cpick.shape, -1, jnp.int32)
    cpick[pl.ds(0, classes), pl.ds(0, capc)] = csrc[0] - (device - 1) * cb
    cpick[pl.ds(classes, classes), pl.ds(0, capc)] = ctgt[0]
    cwin[pl.ds(3 * cb, cwin.shape[0] - 3 * cb)] = jnp.zeros((cwin.shape[0] - 3 * cb, coeffs), BF)

    def coarse_counts(r, _):
        targets = onehot(cb, cpick[pl.ds(classes + r, 1), :])
        sources = onehot(cwin.shape[0], cpick[pl.ds(r, 1), :])
        ccoarse[pl.ds(pl.multiple_of(r * cb, cb), cb)] = dot_nt(targets, sources).astype(BF)
        return 0

    lax.fori_loop(0, classes, coarse_counts, 0)
    lax.fori_loop(0, classes // 2, fine_counts, 0)

    for copy in posts:
        copy.wait_recv()
    rows = lists[...].T[: 2 * classes]
    offset = rows[:classes] - (row - 1) * seg
    which = jnp.where(offset >= seg, 1, 0) + jnp.where(offset >= 2 * seg, 1, 0)
    inside = offset - which * seg - core * half
    inside = jnp.where((inside >= 0) & (inside < half), which * half + inside, -1)
    tpick[pl.ds(0, classes)] = inside
    tpick[pl.ds(classes, classes)] = rows[classes:] - x * quarter

    def top_counts(r, _):
        targets = onehot(quarter, tpick[pl.ds(classes + r, 1), :])
        sources = onehot(3 * half, tpick[pl.ds(r, 1), :])
        ctop[pl.ds(pl.multiple_of(r * quarter, quarter), quarter)] = dot_nt(targets, sources).astype(BF)
        return 0

    lax.fori_loop(0, classes, top_counts, 0)

    def class_columns(r):
        return pl.ds(pl.multiple_of(r * coeffs, coeffs), coeffs)

    moves[6].wait()
    windows[0].wait_recv()
    windows[1].wait_recv()

    def top_rows(r, _):
        counts = ctop[pl.ds(pl.multiple_of(r * quarter, quarter), quarter)]
        hi, lo = split(dot(counts, twin[...]))
        atop[pl.ds(0, quarter), class_columns(r)] = hi
        atop[pl.ds(quarter, quarter), class_columns(r)] = lo
        return 0

    lax.fori_loop(0, classes, top_rows, 0)
    moves[8].wait()
    part = dot(atop[...], ops[...].reshape(classes * coeffs, coeffs))
    part = part[:quarter] + part[quarter:]
    lanes = coeffs // 2
    left = part[:, :lanes].reshape(quarter // 8, 8, lanes)
    right = part[:, lanes:].reshape(quarter // 8, 8, lanes)
    low = lax.broadcasted_iota(jnp.int32, left.shape, 1) < 4
    even = jnp.where(low, left, pltpu.roll(right, 4, 1))
    odd = jnp.where(low, pltpu.roll(left, 4, 1), right)
    for i in range(quarter // 8):
        outbox[2 * i] = even[i]
        outbox[2 * i + 1] = odd[i]
    shares = [
        remote(outbox.at[lax.rem(j + k, planes)], inbox.at[k], rsend.at[k], rrecv.at[k], peer(k))
        for k in range(1, planes)
    ]
    for copy in shares:
        copy.start()
    inbox[0] = outbox[j]

    lax.fori_loop(classes // 2, classes, fine_counts, 0)

    for copy in windows[2:4]:
        copy.wait_recv()
    moves[7].wait()

    def coarse_rows(r, _):
        hi, lo = split(dot(ccoarse[pl.ds(pl.multiple_of(r * cb, cb), cb)], cwin[...]))
        acoarse[pl.ds(0, cb), class_columns(r)] = hi
        acoarse[pl.ds(cb, cb), class_columns(r)] = lo
        return 0

    lax.fori_loop(0, classes, coarse_rows, 0)
    middle = dot(acoarse[...], ops[...].reshape(classes * coeffs, coeffs))
    middle = middle[:cb] + middle[cb:]

    for copy in windows[4:]:
        copy.wait_recv()
    moves[9].wait()
    acc[...] = jnp.zeros_like(acc)

    def fine_rows(r, _):
        acc[...] += dot(dot(cfine[r], fwin[...]).astype(BF), ops[r])
        return 0

    lax.fori_loop(0, classes, fine_rows, 0)

    moves[10].wait()
    for copy in shares:
        copy.wait_recv()
    summed = inbox[0]
    for k in range(1, planes):
        summed += inbox[k]
    top = jnp.concatenate([summed[:4], summed[4:]], axis=1).astype(BF).astype(F32)
    coarse = children(top, l2l[...]) + middle
    coarse = coarse.astype(BF).astype(F32)
    out_ref[...] = children(coarse, l2l[...]) + acc[...]

    for copy in windows + posts + shares:
        copy.wait_send()


def solution(mesh):
    n_row, n_col = mesh.shape["row"], mesh.shape["col"]
    mates = XS * CORES
    planes = n_col // XS

    def per_device(*args):
        top, coarse, fine, m2l, l2l, tsrc, ttgt, csrc, ctgt, fsrc, ftgt = args
        classes, coeffs = m2l.shape[0], m2l.shape[1]
        seg, cb, b = top.shape[0], coarse.shape[0], fine.shape[0]
        quarter = seg // XS
        capt = tsrc.shape[2]
        pad = 128
        slots = -(-mates * capt // pad) * pad
        crows = -(-3 * cb // pad) * pad
        scratch = [
            pltpu.VMEM((3 * seg // CORES, coeffs), BF),
            pltpu.VMEM((crows, coeffs), BF),
            pltpu.VMEM((3 * b, coeffs), BF),
            pltpu.VMEM(m2l.shape, BF),
            pltpu.VMEM(l2l.shape, BF),
            *[pltpu.VMEM(a.shape, jnp.int32) for a in (tsrc, ttgt, csrc, ctgt, fsrc, ftgt)],
            pltpu.VMEM((pad, pad), jnp.int32),
            pltpu.VMEM((capt, pad), jnp.int32),
            pltpu.VMEM((slots, pad), jnp.int32),
            pltpu.VMEM((2 * classes, slots), jnp.int32),
            pltpu.VMEM((2 * classes, pad), jnp.int32),
            pltpu.VMEM((classes * quarter, 3 * seg // CORES), BF),
            pltpu.VMEM((classes * cb, crows), BF),
            pltpu.VMEM((classes, b, 3 * b), BF),
            pltpu.VMEM((2 * quarter, classes * coeffs), BF),
            pltpu.VMEM((2 * cb, classes * coeffs), BF),
            pltpu.VMEM((b, coeffs), F32),
            pltpu.VMEM((planes, 8, coeffs // 2), F32),
            pltpu.VMEM((planes, 8, coeffs // 2), F32),
            pltpu.SemaphoreType.DMA((11,)),
            pltpu.SemaphoreType.DMA((6,)),
            pltpu.SemaphoreType.DMA((6,)),
            pltpu.SemaphoreType.DMA((mates,)),
            pltpu.SemaphoreType.DMA((mates,)),
            pltpu.SemaphoreType.DMA((planes,)),
            pltpu.SemaphoreType.DMA((planes,)),
        ]
        return pl.pallas_call(
            functools.partial(kernel, n_row, n_col),
            out_shape=jax.ShapeDtypeStruct((b, coeffs), F32),
            in_specs=[pl.BlockSpec(memory_space=pl.ANY)] * len(args),
            out_specs=pl.BlockSpec(memory_space=pltpu.VMEM),
            scratch_shapes=scratch,
            compiler_params=pltpu.CompilerParams(
                collective_id=0, has_side_effects=True, vmem_limit_bytes=40 * 1024 * 1024
            ),
        )(*args)

    both = P(("row", "col"), None)
    lists = P(("row", "col"), None, None)
    in_specs = (P("row", None), both, both, P(), P()) + (lists,) * 6
    return jax.shard_map(per_device, mesh=mesh, in_specs=in_specs, out_specs=both, check_vma=False)
```

```python
import functools

import jax
import jax.numpy as jnp
from jax import lax
from jax.experimental import pallas as pl
from jax.experimental.pallas import tpu as pltpu
from jax.sharding import PartitionSpec as P

CORES = 2
XS = 4
MESH = pl.DeviceIdType.MESH
BF = jnp.bfloat16
F32 = jnp.float32


def onehot(rows, picks):
    number = lax.broadcasted_iota(jnp.int32, (rows, picks.shape[1]), 0)
    return jnp.where(number == picks, 1.0, 0.0).astype(BF)


def dot(a, b):
    return jnp.dot(a, b, preferred_element_type=F32)


def dot_nt(a, b):
    return lax.dot_general(a, b, (((1,), (1,)), ((), ())), preferred_element_type=F32)


def split(a):
    hi = a.astype(BF)
    return hi, (a - hi.astype(F32)).astype(BF)


def children(parents, ops):
    n, c = parents.shape
    octants, depth, _ = ops.shape
    rep = jnp.broadcast_to(parents[:, None, :], (n, octants, c)).reshape(n * octants, c)
    which = lax.broadcasted_iota(jnp.int32, (n, octants, c), 1).reshape(n * octants, c)
    parts = [jnp.where(which == o, rep, 0.0).astype(BF) for o in range(octants)]
    return dot(jnp.concatenate(parts, axis=1), ops.reshape(octants * depth, c))


def kernel(
    n_row,
    n_col,
    top_ref,
    coarse_ref,
    fine_ref,
    m2l_ref,
    l2l_ref,
    tsrc_ref,
    ttgt_ref,
    csrc_ref,
    ctgt_ref,
    fsrc_ref,
    ftgt_ref,
    out_ref,
    twin,
    cwin,
    fwin,
    ops,
    l2l,
    tsrc,
    ttgt,
    csrc,
    ctgt,
    fsrc,
    ftgt,
    square,
    mine,
    lists,
    tpick,
    cpick,
    ctop,
    ccoarse,
    cfine,
    atop,
    acoarse,
    acc,
    outbox,
    inbox,
    local_sem,
    wsend,
    wrecv,
    lsend,
    lrecv,
    rsend,
    rrecv,
):
    classes, coeffs = m2l_ref.shape[0], m2l_ref.shape[1]
    seg = top_ref.shape[0]
    half = seg // CORES
    quarter = seg // XS
    cb, b = coarse_ref.shape[0], fine_ref.shape[0]
    capt = tsrc_ref.shape[2]
    capc = csrc_ref.shape[2]
    ys = n_col // (XS * CORES)
    mates = XS * CORES
    planes = ys * CORES

    row, col = lax.axis_index("row"), lax.axis_index("col")
    x, j = col // planes, lax.rem(col, planes)
    y, core = j // CORES, lax.rem(col, CORES)
    device = row * n_col + col
    total = n_row * n_col

    def place(index):
        return (index // n_col, lax.rem(index, n_col))

    after = place(lax.rem(device + 1, total))
    before = place(lax.rem(device + total - 1, total))
    above = (lax.rem(row + 1, n_row), col)
    below = (lax.rem(row + n_row - 1, n_row), col)

    def mate(k):
        m = lax.rem(x * CORES + core + k, mates)
        return (row, (m // CORES) * planes + y * CORES + lax.rem(m, CORES))

    def peer(k):
        return (row, x * planes + lax.rem(j + k, planes))

    barrier = pltpu.get_barrier_semaphore()
    partners = [after, before, above, below]
    partners += [mate(k) for k in range(1, mates)]
    partners += [peer(k) for k in range(1, planes)]
    for partner in partners:
        pl.semaphore_signal(barrier, inc=1, device_id=partner, device_id_type=MESH)

    own_top = top_ref.at[pl.ds(pl.multiple_of(core * half, half), half)]
    moves = [
        (tsrc_ref, tsrc),
        (ttgt_ref, ttgt),
        (fsrc_ref, fsrc),
        (ftgt_ref, ftgt),
        (csrc_ref, csrc),
        (ctgt_ref, ctgt),
        (own_top, twin.at[pl.ds(half, half)]),
        (coarse_ref, cwin.at[pl.ds(cb, cb)]),
        (m2l_ref, ops),
        (fine_ref, fwin.at[pl.ds(b, b)]),
        (l2l_ref, l2l),
    ]
    moves = [pltpu.make_async_copy(s, d, local_sem.at[i]) for i, (s, d) in enumerate(moves)]
    for move in moves:
        move.start()

    square[...] = jnp.zeros_like(square)
    unused = lists.shape[0] - mates * capt
    lists[pl.ds(mates * capt, unused)] = jnp.full((unused, lists.shape[1]), -1, jnp.int32)
    moves[0].wait()
    moves[1].wait()
    square[pl.ds(0, classes), pl.ds(0, capt)] = tsrc[0]
    square[pl.ds(classes, classes), pl.ds(0, capt)] = ttgt[0]
    columns = square[...].T[:capt]
    mine[...] = columns
    lists[pl.ds(0, capt)] = columns

    pl.semaphore_wait(barrier, len(partners))

    def remote(src, dst, send, recv, to):
        return pltpu.make_async_remote_copy(
            src_ref=src, dst_ref=dst, send_sem=send, recv_sem=recv, device_id=to, device_id_type=MESH
        )

    windows = [
        (own_top, twin.at[pl.ds(0, half)], above),
        (own_top, twin.at[pl.ds(2 * half, half)], below),
        (coarse_ref, cwin.at[pl.ds(0, cb)], after),
        (coarse_ref, cwin.at[pl.ds(2 * cb, cb)], before),
        (fine_ref, fwin.at[pl.ds(0, b)], after),
        (fine_ref, fwin.at[pl.ds(2 * b, b)], before),
    ]
    windows = [remote(s, d, wsend.at[i], wrecv.at[i], to) for i, (s, d, to) in enumerate(windows)]
    posts = [
        remote(mine, lists.at[pl.ds(k * capt, capt)], lsend.at[k], lrecv.at[k], mate(k))
        for k in range(1, mates)
    ]
    for copy in windows[:2] + posts + windows[2:]:
        copy.start()

    for i in (2, 3, 4, 5):
        moves[i].wait()

    def fine_counts(r, _):
        targets = onehot(b, ftgt[0, pl.ds(r, 1), :])
        sources = onehot(3 * b, fsrc[0, pl.ds(r, 1), :])
        cfine[r] = dot_nt(targets, sources).astype(BF)
        return 0

    cpick[...] = jnp.full(cpick.shape, -1, jnp.int32)
    cpick[pl.ds(0, classes), pl.ds(0, capc)] = csrc[0] - (device - 1) * cb
    cpick[pl.ds(classes, classes), pl.ds(0, capc)] = ctgt[0]
    cwin[pl.ds(3 * cb, cwin.shape[0] - 3 * cb)] = jnp.zeros((cwin.shape[0] - 3 * cb, coeffs), BF)

    def coarse_counts(r, _):
        targets = onehot(cb, cpick[pl.ds(classes + r, 1), :])
        sources = onehot(cwin.shape[0], cpick[pl.ds(r, 1), :])
        ccoarse[pl.ds(pl.multiple_of(r * cb, cb), cb)] = dot_nt(targets, sources).astype(BF)
        return 0

    lax.fori_loop(0, classes, coarse_counts, 0, unroll=True)
    lax.fori_loop(0, classes // 2, fine_counts, 0, unroll=True)

    for copy in posts:
        copy.wait_recv()
    rows = lists[...].T[: 2 * classes]
    offset = rows[:classes] - (row - 1) * seg
    which = jnp.where(offset >= seg, 1, 0) + jnp.where(offset >= 2 * seg, 1, 0)
    inside = offset - which * seg - core * half
    inside = jnp.where((inside >= 0) & (inside < half), which * half + inside, -1)
    tpick[pl.ds(0, classes)] = inside
    tpick[pl.ds(classes, classes)] = rows[classes:] - x * quarter

    def top_counts(r, _):
        targets = onehot(quarter, tpick[pl.ds(classes + r, 1), :])
        sources = onehot(3 * half, tpick[pl.ds(r, 1), :])
        ctop[pl.ds(pl.multiple_of(r * quarter, quarter), quarter)] = dot_nt(targets, sources).astype(BF)
        return 0

    lax.fori_loop(0, classes, top_counts, 0, unroll=True)

    def class_columns(r):
        return pl.ds(r * coeffs, coeffs)

    moves[6].wait()
    windows[0].wait_recv()
    windows[1].wait_recv()

    hi, lo = split(dot(ctop[...], twin[...]))
    for r in range(classes):
        atop[pl.ds(0, quarter), class_columns(r)] = hi[r * quarter : (r + 1) * quarter]
        atop[pl.ds(quarter, quarter), class_columns(r)] = lo[r * quarter : (r + 1) * quarter]
    moves[8].wait()
    part = dot(atop[...], ops[...].reshape(classes * coeffs, coeffs))
    part = part[:quarter] + part[quarter:]
    lanes = coeffs // 2
    left = part[:, :lanes].reshape(quarter // 8, 8, lanes)
    right = part[:, lanes:].reshape(quarter // 8, 8, lanes)
    low = lax.broadcasted_iota(jnp.int32, left.shape, 1) < 4
    even = jnp.where(low, left, pltpu.roll(right, 4, 1))
    odd = jnp.where(low, pltpu.roll(left, 4, 1), right)
    for i in range(quarter // 8):
        outbox[2 * i] = even[i]
        outbox[2 * i + 1] = odd[i]
    shares = [
        remote(outbox.at[lax.rem(j + k, planes)], inbox.at[k], rsend.at[k], rrecv.at[k], peer(k))
        for k in range(1, planes)
    ]
    for copy in shares:
        copy.start()
    inbox[0] = outbox[j]

    lax.fori_loop(classes // 2, classes, fine_counts, 0, unroll=True)

    for copy in windows[2:4]:
        copy.wait_recv()
    moves[7].wait()

    hi, lo = split(dot(ccoarse[...], cwin[...]))
    for r in range(classes):
        acoarse[pl.ds(0, cb), class_columns(r)] = hi[r * cb : (r + 1) * cb]
        acoarse[pl.ds(cb, cb), class_columns(r)] = lo[r * cb : (r + 1) * cb]
    middle = dot(acoarse[...], ops[...].reshape(classes * coeffs, coeffs))
    middle = middle[:cb] + middle[cb:]

    for copy in windows[4:]:
        copy.wait_recv()
    moves[9].wait()
    acc[...] = jnp.zeros_like(acc)

    def fine_rows(r, _):
        acc[...] += dot(dot(cfine[r], fwin[...]).astype(BF), ops[r])
        return 0

    lax.fori_loop(0, classes, fine_rows, 0, unroll=True)

    moves[10].wait()
    for copy in shares:
        copy.wait_recv()
    summed = inbox[0]
    for k in range(1, planes):
        summed += inbox[k]
    top = jnp.concatenate([summed[:4], summed[4:]], axis=1).astype(BF).astype(F32)
    coarse = children(top, l2l[...]) + middle
    coarse = coarse.astype(BF).astype(F32)
    out_ref[...] = children(coarse, l2l[...]) + acc[...]

    for copy in windows + posts + shares:
        copy.wait_send()


def solution(mesh):
    n_row, n_col = mesh.shape["row"], mesh.shape["col"]
    mates = XS * CORES
    planes = n_col // XS

    def per_device(*args):
        top, coarse, fine, m2l, l2l, tsrc, ttgt, csrc, ctgt, fsrc, ftgt = args
        classes, coeffs = m2l.shape[0], m2l.shape[1]
        seg, cb, b = top.shape[0], coarse.shape[0], fine.shape[0]
        quarter = seg // XS
        capt = tsrc.shape[2]
        pad = 128
        slots = -(-mates * capt // pad) * pad
        crows = -(-3 * cb // pad) * pad
        scratch = [
            pltpu.VMEM((3 * seg // CORES, coeffs), BF),
            pltpu.VMEM((crows, coeffs), BF),
            pltpu.VMEM((3 * b, coeffs), BF),
            pltpu.VMEM(m2l.shape, BF),
            pltpu.VMEM(l2l.shape, BF),
            *[pltpu.VMEM(a.shape, jnp.int32) for a in (tsrc, ttgt, csrc, ctgt, fsrc, ftgt)],
            pltpu.VMEM((pad, pad), jnp.int32),
            pltpu.VMEM((capt, pad), jnp.int32),
            pltpu.VMEM((slots, pad), jnp.int32),
            pltpu.VMEM((2 * classes, slots), jnp.int32),
            pltpu.VMEM((2 * classes, pad), jnp.int32),
            pltpu.VMEM((classes * quarter, 3 * seg // CORES), BF),
            pltpu.VMEM((classes * cb, crows), BF),
            pltpu.VMEM((classes, b, 3 * b), BF),
            pltpu.VMEM((2 * quarter, classes * coeffs), BF),
            pltpu.VMEM((2 * cb, classes * coeffs), BF),
            pltpu.VMEM((b, coeffs), F32),
            pltpu.VMEM((planes, 8, coeffs // 2), F32),
            pltpu.VMEM((planes, 8, coeffs // 2), F32),
            pltpu.SemaphoreType.DMA((11,)),
            pltpu.SemaphoreType.DMA((6,)),
            pltpu.SemaphoreType.DMA((6,)),
            pltpu.SemaphoreType.DMA((mates,)),
            pltpu.SemaphoreType.DMA((mates,)),
            pltpu.SemaphoreType.DMA((planes,)),
            pltpu.SemaphoreType.DMA((planes,)),
        ]
        return pl.pallas_call(
            functools.partial(kernel, n_row, n_col),
            out_shape=jax.ShapeDtypeStruct((b, coeffs), F32),
            in_specs=[pl.BlockSpec(memory_space=pltpu.HBM)] * len(args),
            out_specs=pl.BlockSpec(memory_space=pltpu.VMEM),
            scratch_shapes=scratch,
            compiler_params=pltpu.CompilerParams(
                collective_id=0, has_side_effects=True, vmem_limit_bytes=56 * 1024 * 1024
            ),
        )(*args)

    both = P(("row", "col"), None)
    lists = P(("row", "col"), None, None)
    in_specs = (P("row", None), both, both, P(), P()) + (lists,) * 6
    return jax.shard_map(per_device, mesh=mesh, in_specs=in_specs, out_specs=both, check_vma=False)
```

```python
import functools

import jax
import jax.numpy as jnp
from jax import lax
from jax.experimental import pallas as pl
from jax.experimental.pallas import tpu as pltpu
from jax.sharding import PartitionSpec as P

CORES = 2
XS = 4
EARLY = 12
MIDDLE = 16
MESH = pl.DeviceIdType.MESH
BF = jnp.bfloat16
F32 = jnp.float32


def onehot(rows, picks):
    number = lax.broadcasted_iota(jnp.int32, (rows, picks.shape[1]), 0)
    return jnp.where(number == picks, 1.0, 0.0).astype(BF)


def dot(a, b):
    return jnp.dot(a, b, preferred_element_type=F32)


def dot_nt(a, b):
    return lax.dot_general(a, b, (((1,), (1,)), ((), ())), preferred_element_type=F32)


def split(a):
    hi = a.astype(BF)
    return hi, (a - hi.astype(F32)).astype(BF)


def children(parents, ops):
    n, c = parents.shape
    octants, depth, _ = ops.shape
    rep = jnp.broadcast_to(parents[:, None, :], (n, octants, c)).reshape(n * octants, c)
    which = lax.broadcasted_iota(jnp.int32, (n, octants, c), 1).reshape(n * octants, c)
    parts = [jnp.where(which == o, rep, 0.0).astype(BF) for o in range(octants)]
    return dot(jnp.concatenate(parts, axis=1), ops.reshape(octants * depth, c))


def kernel(
    n_row,
    n_col,
    top_ref,
    coarse_ref,
    fine_ref,
    m2l_ref,
    l2l_ref,
    tsrc_ref,
    ttgt_ref,
    csrc_ref,
    ctgt_ref,
    fsrc_ref,
    ftgt_ref,
    out_ref,
    twin,
    cwin,
    fwin,
    ops,
    l2l,
    tsrc,
    ttgt,
    csrc,
    ctgt,
    fsrc,
    ftgt,
    square,
    mine,
    lists,
    tpick,
    cpick,
    ctop,
    ccoarse,
    cfine,
    atop,
    acoarse,
    acc,
    outbox,
    inbox,
    local_sem,
    wsend,
    wrecv,
    lsend,
    lrecv,
    rsend,
    rrecv,
):
    classes, coeffs = m2l_ref.shape[0], m2l_ref.shape[1]
    seg = top_ref.shape[0]
    half = seg // CORES
    quarter = seg // XS
    cb, b = coarse_ref.shape[0], fine_ref.shape[0]
    capt = tsrc_ref.shape[2]
    capc = csrc_ref.shape[2]
    ys = n_col // (XS * CORES)
    mates = XS * CORES
    planes = ys * CORES

    row, col = lax.axis_index("row"), lax.axis_index("col")
    x, j = col // planes, lax.rem(col, planes)
    y, core = j // CORES, lax.rem(col, CORES)
    device = row * n_col + col
    total = n_row * n_col

    def place(index):
        return (index // n_col, lax.rem(index, n_col))

    after = place(lax.rem(device + 1, total))
    before = place(lax.rem(device + total - 1, total))
    above = (lax.rem(row + 1, n_row), col)
    below = (lax.rem(row + n_row - 1, n_row), col)

    def mate(k):
        m = lax.rem(x * CORES + core + k, mates)
        return (row, (m // CORES) * planes + y * CORES + lax.rem(m, CORES))

    def peer(k):
        return (row, x * planes + lax.rem(j + k, planes))

    barrier = pltpu.get_barrier_semaphore()
    partners = [mate(k) for k in range(1, mates)]
    partners += [peer(k) for k in range(1, planes)]
    for partner in partners:
        pl.semaphore_signal(barrier, inc=1, device_id=partner, device_id_type=MESH)
    has_above, has_below = row < n_row - 1, row > 0
    has_after, has_before = device < total - 1, device > 0
    expected = len(partners)
    edges = [(has_above, above), (has_below, below), (has_after, after), (has_before, before)]
    for there, partner in edges:
        expected += jnp.where(there, 1, 0)

        @pl.when(there)
        def _(partner=partner):
            pl.semaphore_signal(barrier, inc=1, device_id=partner, device_id_type=MESH)

    own_top = top_ref.at[pl.ds(pl.multiple_of(core * half, half), half)]
    moves = [
        (tsrc_ref, tsrc),
        (ttgt_ref, ttgt),
        (fsrc_ref, fsrc),
        (ftgt_ref, ftgt),
        (csrc_ref, csrc),
        (ctgt_ref, ctgt),
        (own_top, twin.at[pl.ds(half, half)]),
        (coarse_ref, cwin.at[pl.ds(cb, cb)]),
        (m2l_ref, ops),
        (fine_ref, fwin.at[pl.ds(b, b)]),
        (l2l_ref, l2l),
    ]
    moves = [pltpu.make_async_copy(s, d, local_sem.at[i]) for i, (s, d) in enumerate(moves)]
    for move in moves:
        move.start()

    square[...] = jnp.zeros_like(square)
    unused = lists.shape[0] - mates * capt
    lists[pl.ds(mates * capt, unused)] = jnp.full((unused, lists.shape[1]), -1, jnp.int32)
    moves[0].wait()
    moves[1].wait()
    square[pl.ds(0, classes), pl.ds(0, capt)] = tsrc[0]
    square[pl.ds(classes, classes), pl.ds(0, capt)] = ttgt[0]
    columns = square[...].T[:capt]
    mine[...] = columns
    lists[pl.ds(0, capt)] = columns

    def fine_counts(r, _):
        targets = onehot(b, ftgt[0, pl.ds(r, 1), :])
        sources = onehot(3 * b, fsrc[0, pl.ds(r, 1), :])
        cfine[r] = dot_nt(targets, sources).astype(BF)
        return 0

    moves[2].wait()
    moves[3].wait()
    lax.fori_loop(0, EARLY, fine_counts, 0, unroll=True)

    pl.semaphore_wait(barrier, expected)

    def remote(src, dst, send, recv, to):
        return pltpu.make_async_remote_copy(
            src_ref=src, dst_ref=dst, send_sem=send, recv_sem=recv, device_id=to, device_id_type=MESH
        )

    windows = [
        (own_top, twin.at[pl.ds(0, half)], above, has_above, has_below),
        (own_top, twin.at[pl.ds(2 * half, half)], below, has_below, has_above),
        (coarse_ref, cwin.at[pl.ds(0, cb)], after, has_after, has_before),
        (coarse_ref, cwin.at[pl.ds(2 * cb, cb)], before, has_before, has_after),
        (fine_ref, fwin.at[pl.ds(0, b)], after, has_after, has_before),
        (fine_ref, fwin.at[pl.ds(2 * b, b)], before, has_before, has_after),
    ]
    windows = [
        (remote(s, d, wsend.at[i], wrecv.at[i], to), d, sent, received)
        for i, (s, d, to, sent, received) in enumerate(windows)
    ]

    def start(window):
        pl.when(window[2])(window[0].start)

    def receive(window):
        pl.when(window[3])(window[0].wait_recv)

    posts = [
        remote(mine, lists.at[pl.ds(k * capt, capt)], lsend.at[k], lrecv.at[k], mate(k))
        for k in range(1, mates)
    ]
    for window in windows[:2]:
        start(window)
    for copy in posts:
        copy.start()
    for window in windows[2:]:
        start(window)
    for _, there, _, received in windows:

        @pl.when(jnp.logical_not(received))
        def _(there=there):
            there[...] = jnp.zeros(there.shape, BF)

    moves[4].wait()
    moves[5].wait()
    cpick[...] = jnp.full(cpick.shape, -1, jnp.int32)
    cpick[pl.ds(0, classes), pl.ds(0, capc)] = csrc[0] - (device - 1) * cb
    cpick[pl.ds(classes, classes), pl.ds(0, capc)] = ctgt[0]
    cwin[pl.ds(3 * cb, cwin.shape[0] - 3 * cb)] = jnp.zeros((cwin.shape[0] - 3 * cb, coeffs), BF)

    def coarse_counts(r, _):
        targets = onehot(cb, cpick[pl.ds(classes + r, 1), :])
        sources = onehot(cwin.shape[0], cpick[pl.ds(r, 1), :])
        ccoarse[pl.ds(pl.multiple_of(r * cb, cb), cb)] = dot_nt(targets, sources).astype(BF)
        return 0

    lax.fori_loop(0, classes, coarse_counts, 0, unroll=True)
    lax.fori_loop(EARLY, MIDDLE, fine_counts, 0, unroll=True)

    for copy in posts:
        copy.wait_recv()
    rows = lists[...].T[: 2 * classes]
    offset = rows[:classes] - (row - 1) * seg
    which = jnp.where(offset >= seg, 1, 0) + jnp.where(offset >= 2 * seg, 1, 0)
    inside = offset - which * seg - core * half
    inside = jnp.where((inside >= 0) & (inside < half), which * half + inside, -1)
    tpick[pl.ds(0, classes)] = inside
    tpick[pl.ds(classes, classes)] = rows[classes:] - x * quarter

    def top_counts(r, _):
        targets = onehot(quarter, tpick[pl.ds(classes + r, 1), :])
        sources = onehot(3 * half, tpick[pl.ds(r, 1), :])
        ctop[pl.ds(pl.multiple_of(r * quarter, quarter), quarter)] = dot_nt(targets, sources).astype(BF)
        return 0

    lax.fori_loop(0, classes, top_counts, 0, unroll=True)

    def class_columns(r):
        return pl.ds(r * coeffs, coeffs)

    moves[6].wait()
    receive(windows[0])
    receive(windows[1])

    hi, lo = split(dot(ctop[...], twin[...]))
    for r in range(classes):
        atop[pl.ds(0, quarter), class_columns(r)] = hi[r * quarter : (r + 1) * quarter]
        atop[pl.ds(quarter, quarter), class_columns(r)] = lo[r * quarter : (r + 1) * quarter]
    moves[8].wait()
    part = dot(atop[...], ops[...].reshape(classes * coeffs, coeffs))
    part = part[:quarter] + part[quarter:]
    lanes = coeffs // 2
    left = part[:, :lanes].reshape(quarter // 8, 8, lanes)
    right = part[:, lanes:].reshape(quarter // 8, 8, lanes)
    low = lax.broadcasted_iota(jnp.int32, left.shape, 1) < 4
    even = jnp.where(low, left, pltpu.roll(right, 4, 1))
    odd = jnp.where(low, pltpu.roll(left, 4, 1), right)
    for i in range(quarter // 8):
        outbox[2 * i] = even[i]
        outbox[2 * i + 1] = odd[i]
    shares = [
        remote(outbox.at[lax.rem(j + k, planes)], inbox.at[k], rsend.at[k], rrecv.at[k], peer(k))
        for k in range(1, planes)
    ]
    for copy in shares:
        copy.start()
    inbox[0] = outbox[j]

    lax.fori_loop(MIDDLE, classes, fine_counts, 0, unroll=True)

    for window in windows[2:4]:
        receive(window)
    moves[7].wait()

    hi, lo = split(dot(ccoarse[...], cwin[...]))
    for r in range(classes):
        acoarse[pl.ds(0, cb), class_columns(r)] = hi[r * cb : (r + 1) * cb]
        acoarse[pl.ds(cb, cb), class_columns(r)] = lo[r * cb : (r + 1) * cb]
    middle = dot(acoarse[...], ops[...].reshape(classes * coeffs, coeffs))
    middle = middle[:cb] + middle[cb:]

    for window in windows[4:]:
        receive(window)
    moves[9].wait()
    acc[...] = jnp.zeros_like(acc)

    def fine_rows(r, _):
        acc[...] += dot(dot(cfine[r], fwin[...]).astype(BF), ops[r])
        return 0

    lax.fori_loop(0, classes, fine_rows, 0, unroll=True)

    moves[10].wait()
    for copy in shares:
        copy.wait_recv()
    summed = inbox[0]
    for k in range(1, planes):
        summed += inbox[k]
    top = jnp.concatenate([summed[:4], summed[4:]], axis=1).astype(BF).astype(F32)
    coarse = children(top, l2l[...]) + middle
    coarse = coarse.astype(BF).astype(F32)
    out_ref[...] = children(coarse, l2l[...]) + acc[...]

    for window in windows:
        pl.when(window[2])(window[0].wait_send)
    for copy in posts + shares:
        copy.wait_send()


def solution(mesh):
    n_row, n_col = mesh.shape["row"], mesh.shape["col"]
    mates = XS * CORES
    planes = n_col // XS

    def per_device(*args):
        top, coarse, fine, m2l, l2l, tsrc, ttgt, csrc, ctgt, fsrc, ftgt = args
        classes, coeffs = m2l.shape[0], m2l.shape[1]
        seg, cb, b = top.shape[0], coarse.shape[0], fine.shape[0]
        quarter = seg // XS
        capt = tsrc.shape[2]
        pad = 128
        slots = -(-mates * capt // pad) * pad
        crows = -(-3 * cb // pad) * pad
        scratch = [
            pltpu.VMEM((3 * seg // CORES, coeffs), BF),
            pltpu.VMEM((crows, coeffs), BF),
            pltpu.VMEM((3 * b, coeffs), BF),
            pltpu.VMEM(m2l.shape, BF),
            pltpu.VMEM(l2l.shape, BF),
            *[pltpu.VMEM(a.shape, jnp.int32) for a in (tsrc, ttgt, csrc, ctgt, fsrc, ftgt)],
            pltpu.VMEM((pad, pad), jnp.int32),
            pltpu.VMEM((capt, pad), jnp.int32),
            pltpu.VMEM((slots, pad), jnp.int32),
            pltpu.VMEM((2 * classes, slots), jnp.int32),
            pltpu.VMEM((2 * classes, pad), jnp.int32),
            pltpu.VMEM((classes * quarter, 3 * seg // CORES), BF),
            pltpu.VMEM((classes * cb, crows), BF),
            pltpu.VMEM((classes, b, 3 * b), BF),
            pltpu.VMEM((2 * quarter, classes * coeffs), BF),
            pltpu.VMEM((2 * cb, classes * coeffs), BF),
            pltpu.VMEM((b, coeffs), F32),
            pltpu.VMEM((planes, 8, coeffs // 2), F32),
            pltpu.VMEM((planes, 8, coeffs // 2), F32),
            pltpu.SemaphoreType.DMA((11,)),
            pltpu.SemaphoreType.DMA((6,)),
            pltpu.SemaphoreType.DMA((6,)),
            pltpu.SemaphoreType.DMA((mates,)),
            pltpu.SemaphoreType.DMA((mates,)),
            pltpu.SemaphoreType.DMA((planes,)),
            pltpu.SemaphoreType.DMA((planes,)),
        ]
        return pl.pallas_call(
            functools.partial(kernel, n_row, n_col),
            out_shape=jax.ShapeDtypeStruct((b, coeffs), F32),
            in_specs=[pl.BlockSpec(memory_space=pltpu.HBM)] * len(args),
            out_specs=pl.BlockSpec(memory_space=pltpu.VMEM),
            scratch_shapes=scratch,
            compiler_params=pltpu.CompilerParams(
                collective_id=0, has_side_effects=True, vmem_limit_bytes=56 * 1024 * 1024
            ),
        )(*args)

    both = P(("row", "col"), None)
    lists = P(("row", "col"), None, None)
    in_specs = (P("row", None), both, both, P(), P()) + (lists,) * 6
    return jax.shard_map(per_device, mesh=mesh, in_specs=in_specs, out_specs=both, check_vma=False)
```

```python
import functools

import jax
import jax.numpy as jnp
from jax import lax
from jax.experimental import pallas as pl
from jax.experimental.pallas import tpu as pltpu
from jax.sharding import PartitionSpec as P

CORES = 2
XS = 4
EARLY = 12
MIDDLE = 16
MESH = pl.DeviceIdType.MESH
BF = jnp.bfloat16
F32 = jnp.float32


def onehot(rows, picks):
    number = lax.broadcasted_iota(jnp.int32, (rows, picks.shape[1]), 0)
    return jnp.where(number == picks, 1.0, 0.0).astype(BF)


def dot(a, b):
    return jnp.dot(a, b, preferred_element_type=F32)


def dot_nt(a, b):
    return lax.dot_general(a, b, (((1,), (1,)), ((), ())), preferred_element_type=F32)


def split(a):
    hi = a.astype(BF)
    return hi, (a - hi.astype(F32)).astype(BF)


def children(parents, ops):
    n, c = parents.shape
    octants, depth, _ = ops.shape
    rep = jnp.broadcast_to(parents[:, None, :], (n, octants, c)).reshape(n * octants, c)
    which = lax.broadcasted_iota(jnp.int32, (n, octants, c), 1).reshape(n * octants, c)
    parts = [jnp.where(which == o, rep, 0.0).astype(BF) for o in range(octants)]
    return dot(jnp.concatenate(parts, axis=1), ops.reshape(octants * depth, c))


def kernel(
    n_row,
    n_col,
    top_ref,
    coarse_ref,
    fine_ref,
    m2l_ref,
    l2l_ref,
    tsrc_ref,
    ttgt_ref,
    csrc_ref,
    ctgt_ref,
    fsrc_ref,
    ftgt_ref,
    out_ref,
    twin,
    cwin,
    fwin,
    ops,
    l2l,
    tsrc,
    ttgt,
    csrc,
    ctgt,
    fsrc,
    ftgt,
    square,
    mine,
    lists,
    tpick,
    cpick,
    ctop,
    ccoarse,
    cfine,
    atop,
    acoarse,
    acc,
    outbox,
    inbox,
    local_sem,
    wsend,
    wrecv,
    lsend,
    lrecv,
    rsend,
    rrecv,
):
    classes, coeffs = m2l_ref.shape[0], m2l_ref.shape[1]
    seg = top_ref.shape[0]
    half = seg // CORES
    quarter = seg // XS
    cb, b = coarse_ref.shape[0], fine_ref.shape[0]
    capt = tsrc_ref.shape[2]
    capc = csrc_ref.shape[2]
    ys = n_col // (XS * CORES)
    mates = XS * CORES
    planes = ys * CORES

    row, col = lax.axis_index("row"), lax.axis_index("col")
    x, j = col // planes, lax.rem(col, planes)
    y, core = j // CORES, lax.rem(col, CORES)
    device = row * n_col + col
    total = n_row * n_col

    def place(index):
        return (index // n_col, lax.rem(index, n_col))

    after = place(lax.rem(device + 1, total))
    before = place(lax.rem(device + total - 1, total))
    above = (lax.rem(row + 1, n_row), col)
    below = (lax.rem(row + n_row - 1, n_row), col)

    def mate(k):
        m = lax.rem(x * CORES + core + k, mates)
        return (row, (m // CORES) * planes + y * CORES + lax.rem(m, CORES))

    def peer(k):
        return (row, x * planes + lax.rem(j + k, planes))

    own_top = top_ref.at[pl.ds(pl.multiple_of(core * half, half), half)]
    moves = [
        (tsrc_ref, tsrc),
        (ttgt_ref, ttgt),
        (fsrc_ref, fsrc),
        (ftgt_ref, ftgt),
        (csrc_ref, csrc),
        (ctgt_ref, ctgt),
        (own_top, twin.at[pl.ds(half, half)]),
        (coarse_ref, cwin.at[pl.ds(cb, cb)]),
        (m2l_ref, ops),
        (fine_ref, fwin.at[pl.ds(b, b)]),
        (l2l_ref, l2l),
    ]
    moves = [pltpu.make_async_copy(s, d, local_sem.at[i]) for i, (s, d) in enumerate(moves)]
    for move in moves[:4]:
        move.start()

    barrier = pltpu.get_barrier_semaphore()
    mate_order = sorted(range(1, mates), key=lambda k: -min(k, mates - k))
    peer_order = sorted(range(1, planes), key=lambda k: -min(k, planes - k))
    partners = [peer(k) for k in peer_order] + [mate(k) for k in mate_order]
    for partner in partners:
        pl.semaphore_signal(barrier, inc=1, device_id=partner, device_id_type=MESH)
    has_above, has_below = row < n_row - 1, row > 0
    has_after, has_before = device < total - 1, device > 0
    expected = len(partners)
    edges = [(has_above, above), (has_below, below), (has_after, after), (has_before, before)]
    for there, partner in edges:
        expected += jnp.where(there, 1, 0)

        @pl.when(there)
        def _(partner=partner):
            pl.semaphore_signal(barrier, inc=1, device_id=partner, device_id_type=MESH)

    for move in moves[4:]:
        move.start()

    square[...] = jnp.zeros_like(square)
    unused = lists.shape[0] - mates * capt
    lists[pl.ds(mates * capt, unused)] = jnp.full((unused, lists.shape[1]), -1, jnp.int32)
    moves[0].wait()
    moves[1].wait()
    square[pl.ds(0, classes), pl.ds(0, capt)] = tsrc[0]
    square[pl.ds(classes, classes), pl.ds(0, capt)] = ttgt[0]
    columns = square[...].T[:capt]
    mine[...] = columns
    lists[pl.ds(0, capt)] = columns

    def fine_counts(r, _):
        targets = onehot(b, ftgt[0, pl.ds(r, 1), :])
        sources = onehot(3 * b, fsrc[0, pl.ds(r, 1), :])
        cfine[r] = dot_nt(targets, sources).astype(BF)
        return 0

    moves[2].wait()
    moves[3].wait()
    lax.fori_loop(0, EARLY, fine_counts, 0, unroll=True)

    pl.semaphore_wait(barrier, expected)

    def remote(src, dst, send, recv, to):
        return pltpu.make_async_remote_copy(
            src_ref=src, dst_ref=dst, send_sem=send, recv_sem=recv, device_id=to, device_id_type=MESH
        )

    windows = [
        (own_top, twin.at[pl.ds(0, half)], above, has_above, has_below),
        (own_top, twin.at[pl.ds(2 * half, half)], below, has_below, has_above),
        (coarse_ref, cwin.at[pl.ds(0, cb)], after, has_after, has_before),
        (coarse_ref, cwin.at[pl.ds(2 * cb, cb)], before, has_before, has_after),
        (fine_ref, fwin.at[pl.ds(0, b)], after, has_after, has_before),
        (fine_ref, fwin.at[pl.ds(2 * b, b)], before, has_before, has_after),
    ]
    windows = [
        (remote(s, d, wsend.at[i], wrecv.at[i], to), d, sent, received)
        for i, (s, d, to, sent, received) in enumerate(windows)
    ]

    def start(window):
        pl.when(window[2])(window[0].start)

    def receive(window):
        pl.when(window[3])(window[0].wait_recv)

    posts = [
        remote(mine, lists.at[pl.ds(k * capt, capt)], lsend, lrecv, mate(k))
        for k in mate_order
    ]
    arrived = pl.ds(capt, (mates - 1) * capt)
    all_posts = remote(lists.at[arrived], lists.at[arrived], lsend, lrecv, mate(1))
    for copy in posts:
        copy.start()
    for window in windows:
        start(window)
    for _, there, _, received in windows:

        @pl.when(jnp.logical_not(received))
        def _(there=there):
            there[...] = jnp.zeros(there.shape, BF)

    moves[4].wait()
    moves[5].wait()
    cpick[...] = jnp.full(cpick.shape, -1, jnp.int32)
    cpick[pl.ds(0, classes), pl.ds(0, capc)] = csrc[0] - (device - 1) * cb
    cpick[pl.ds(classes, classes), pl.ds(0, capc)] = ctgt[0]
    cwin[pl.ds(3 * cb, cwin.shape[0] - 3 * cb)] = jnp.zeros((cwin.shape[0] - 3 * cb, coeffs), BF)

    def coarse_counts(r, _):
        targets = onehot(cb, cpick[pl.ds(classes + r, 1), :])
        sources = onehot(cwin.shape[0], cpick[pl.ds(r, 1), :])
        ccoarse[pl.ds(pl.multiple_of(r * cb, cb), cb)] = dot_nt(targets, sources).astype(BF)
        return 0

    lax.fori_loop(0, classes, coarse_counts, 0, unroll=True)
    lax.fori_loop(EARLY, MIDDLE, fine_counts, 0, unroll=True)

    all_posts.wait_recv()
    rows = lists[...].T[: 2 * classes]
    offset = rows[:classes] - (row - 1) * seg
    which = jnp.where(offset >= seg, 1, 0) + jnp.where(offset >= 2 * seg, 1, 0)
    inside = offset - which * seg - core * half
    inside = jnp.where((inside >= 0) & (inside < half), which * half + inside, -1)
    tpick[pl.ds(0, classes)] = inside
    tpick[pl.ds(classes, classes)] = rows[classes:] - x * quarter

    def top_counts(r, _):
        targets = onehot(quarter, tpick[pl.ds(classes + r, 1), :])
        sources = onehot(3 * half, tpick[pl.ds(r, 1), :])
        ctop[pl.ds(pl.multiple_of(r * quarter, quarter), quarter)] = dot_nt(targets, sources).astype(BF)
        return 0

    lax.fori_loop(0, classes, top_counts, 0, unroll=True)

    def class_columns(r):
        return pl.ds(r * coeffs, coeffs)

    moves[6].wait()
    receive(windows[0])
    receive(windows[1])

    hi, lo = split(dot(ctop[...], twin[...]))
    for r in range(classes):
        atop[pl.ds(0, quarter), class_columns(r)] = hi[r * quarter : (r + 1) * quarter]
        atop[pl.ds(quarter, quarter), class_columns(r)] = lo[r * quarter : (r + 1) * quarter]
    moves[8].wait()
    part = dot(atop[...], ops[...].reshape(classes * coeffs, coeffs))
    part = part[:quarter] + part[quarter:]
    lanes = coeffs // 2
    left = part[:, :lanes].reshape(quarter // 8, 8, lanes)
    right = part[:, lanes:].reshape(quarter // 8, 8, lanes)
    low = lax.broadcasted_iota(jnp.int32, left.shape, 1) < 4
    even = jnp.where(low, left, pltpu.roll(right, 4, 1))
    odd = jnp.where(low, pltpu.roll(left, 4, 1), right)
    for i in range(quarter // 8):
        outbox[2 * i] = even[i]
        outbox[2 * i + 1] = odd[i]
    shares = [
        remote(outbox.at[lax.rem(j + k, planes)], inbox.at[k], rsend, rrecv, peer(k))
        for k in peer_order
    ]
    arrived = pl.ds(1, planes - 1)
    all_shares = remote(outbox.at[arrived], inbox.at[arrived], rsend, rrecv, peer(1))
    for copy in shares:
        copy.start()
    inbox[0] = outbox[j]

    lax.fori_loop(MIDDLE, classes, fine_counts, 0, unroll=True)

    for window in windows[2:4]:
        receive(window)
    moves[7].wait()

    hi, lo = split(dot(ccoarse[...], cwin[...]))
    for r in range(classes):
        acoarse[pl.ds(0, cb), class_columns(r)] = hi[r * cb : (r + 1) * cb]
        acoarse[pl.ds(cb, cb), class_columns(r)] = lo[r * cb : (r + 1) * cb]
    middle = dot(acoarse[...], ops[...].reshape(classes * coeffs, coeffs))
    middle = middle[:cb] + middle[cb:]

    for window in windows[4:]:
        receive(window)
    moves[9].wait()
    acc[...] = jnp.zeros_like(acc)

    def fine_rows(r, _):
        acc[...] += dot(dot(cfine[r], fwin[...]).astype(BF), ops[r])
        return 0

    lax.fori_loop(0, classes, fine_rows, 0, unroll=True)

    moves[10].wait()
    for window in windows:
        pl.when(window[2])(window[0].wait_send)
    all_posts.wait_send()
    all_shares.wait_send()
    all_shares.wait_recv()
    summed = inbox[0]
    for k in range(1, planes):
        summed += inbox[k]
    top = jnp.concatenate([summed[:4], summed[4:]], axis=1).astype(BF).astype(F32)
    coarse = children(top, l2l[...]) + middle
    coarse = coarse.astype(BF).astype(F32)
    out_ref[...] = children(coarse, l2l[...]) + acc[...]


def solution(mesh):
    n_row, n_col = mesh.shape["row"], mesh.shape["col"]
    mates = XS * CORES
    planes = n_col // XS

    def per_device(*args):
        top, coarse, fine, m2l, l2l, tsrc, ttgt, csrc, ctgt, fsrc, ftgt = args
        classes, coeffs = m2l.shape[0], m2l.shape[1]
        seg, cb, b = top.shape[0], coarse.shape[0], fine.shape[0]
        quarter = seg // XS
        capt = tsrc.shape[2]
        pad = 128
        slots = -(-mates * capt // pad) * pad
        crows = -(-3 * cb // pad) * pad
        scratch = [
            pltpu.VMEM((3 * seg // CORES, coeffs), BF),
            pltpu.VMEM((crows, coeffs), BF),
            pltpu.VMEM((3 * b, coeffs), BF),
            pltpu.VMEM(m2l.shape, BF),
            pltpu.VMEM(l2l.shape, BF),
            *[pltpu.VMEM(a.shape, jnp.int32) for a in (tsrc, ttgt, csrc, ctgt, fsrc, ftgt)],
            pltpu.VMEM((pad, pad), jnp.int32),
            pltpu.VMEM((capt, pad), jnp.int32),
            pltpu.VMEM((slots, pad), jnp.int32),
            pltpu.VMEM((2 * classes, slots), jnp.int32),
            pltpu.VMEM((2 * classes, pad), jnp.int32),
            pltpu.VMEM((classes * quarter, 3 * seg // CORES), BF),
            pltpu.VMEM((classes * cb, crows), BF),
            pltpu.VMEM((classes, b, 3 * b), BF),
            pltpu.VMEM((2 * quarter, classes * coeffs), BF),
            pltpu.VMEM((2 * cb, classes * coeffs), BF),
            pltpu.VMEM((b, coeffs), F32),
            pltpu.VMEM((planes, 8, coeffs // 2), F32),
            pltpu.VMEM((planes, 8, coeffs // 2), F32),
            pltpu.SemaphoreType.DMA((11,)),
            pltpu.SemaphoreType.DMA((6,)),
            pltpu.SemaphoreType.DMA((6,)),
            pltpu.SemaphoreType.DMA,
            pltpu.SemaphoreType.DMA,
            pltpu.SemaphoreType.DMA,
            pltpu.SemaphoreType.DMA,
        ]
        return pl.pallas_call(
            functools.partial(kernel, n_row, n_col),
            out_shape=jax.ShapeDtypeStruct((b, coeffs), F32),
            in_specs=[pl.BlockSpec(memory_space=pltpu.HBM)] * len(args),
            out_specs=pl.BlockSpec(memory_space=pltpu.VMEM),
            scratch_shapes=scratch,
            compiler_params=pltpu.CompilerParams(
                collective_id=0, has_side_effects=True, vmem_limit_bytes=40 * 1024 * 1024
            ),
        )(*[pltpu.with_memory_space_constraint(a, pltpu.HBM) for a in args])

    both = P(("row", "col"), None)
    lists = P(("row", "col"), None, None)
    in_specs = (P("row", None), both, both, P(), P()) + (lists,) * 6
    return jax.shard_map(per_device, mesh=mesh, in_specs=in_specs, out_specs=both, check_vma=False)
```

```python
import functools

import jax
import jax.numpy as jnp
from jax import lax
from jax.experimental import pallas as pl
from jax.experimental.pallas import tpu as pltpu
from jax.sharding import PartitionSpec as P

CORES = 2
XS = 4
EARLY = 12
MIDDLE = 16
TOGETHER = 4
MESH = pl.DeviceIdType.MESH
BF = jnp.bfloat16
F32 = jnp.float32
F8 = jnp.float8_e4m3fn


def onehot(rows, picks):
    number = lax.broadcasted_iota(jnp.int32, (rows, picks.shape[1]), 0)
    return jnp.where(number == picks, 1.0, 0.0).astype(F8)


def dot(a, b):
    return jnp.dot(a, b, preferred_element_type=F32)


def dot_nt(a, b):
    return lax.dot_general(a, b, (((1,), (1,)), ((), ())), preferred_element_type=F32)


def split(a):
    hi = a.astype(BF)
    return hi, (a - hi.astype(F32)).astype(BF)


def children(parents, ops):
    n, c = parents.shape
    octants, depth, _ = ops.shape
    rep = jnp.broadcast_to(parents[:, None, :], (n, octants, c)).reshape(n * octants, c)
    which = lax.broadcasted_iota(jnp.int32, (n, octants, c), 1).reshape(n * octants, c)
    parts = [jnp.where(which == o, rep, 0.0).astype(BF) for o in range(octants)]
    return dot(jnp.concatenate(parts, axis=1), ops.reshape(octants * depth, c))


def kernel(
    n_row,
    n_col,
    top_ref,
    coarse_ref,
    fine_ref,
    m2l_ref,
    l2l_ref,
    tsrc_ref,
    ttgt_ref,
    csrc_ref,
    ctgt_ref,
    fsrc_ref,
    ftgt_ref,
    out_ref,
    twin,
    cwin,
    fwin,
    ops,
    l2l,
    tsrc,
    ttgt,
    csrc,
    ctgt,
    fsrc,
    ftgt,
    square,
    mine,
    lists,
    tpick,
    cpick,
    ccoarse,
    cfine,
    atop,
    acoarse,
    acc,
    outbox,
    inbox,
    local_sem,
    wsend,
    wrecv,
    lsend,
    lrecv,
    rsend,
    rrecv,
    learnt,
):
    classes, coeffs = m2l_ref.shape[0], m2l_ref.shape[1]
    seg = top_ref.shape[0]
    half = seg // CORES
    quarter = seg // XS
    cb, b = coarse_ref.shape[0], fine_ref.shape[0]
    capt = tsrc_ref.shape[2]
    capc = csrc_ref.shape[2]
    ys = n_col // (XS * CORES)
    mates = XS * CORES
    planes = ys * CORES

    row, col = lax.axis_index("row"), lax.axis_index("col")
    x, j = col // planes, lax.rem(col, planes)
    y, core = j // CORES, lax.rem(col, CORES)
    device = row * n_col + col
    total = n_row * n_col

    def place(index):
        return (index // n_col, lax.rem(index, n_col))

    after = place(lax.rem(device + 1, total))
    before = place(lax.rem(device + total - 1, total))
    above = (lax.rem(row + 1, n_row), col)
    below = (lax.rem(row + n_row - 1, n_row), col)

    def mate(k):
        m = lax.rem(x * CORES + core + k, mates)
        return (row, (m // CORES) * planes + y * CORES + lax.rem(m, CORES))

    def peer(k):
        return (row, x * planes + lax.rem(j + k, planes))

    own_top = top_ref.at[pl.ds(pl.multiple_of(core * half, half), half)]
    moves = [
        (tsrc_ref, tsrc),
        (ttgt_ref, ttgt),
        (fsrc_ref, fsrc),
        (ftgt_ref, ftgt),
        (csrc_ref, csrc),
        (ctgt_ref, ctgt),
        (own_top, twin.at[pl.ds(half, half)]),
        (coarse_ref, cwin.at[pl.ds(cb, cb)]),
        (m2l_ref, ops),
        (fine_ref, fwin.at[pl.ds(b, b)]),
        (l2l_ref, l2l),
    ]
    moves = [pltpu.make_async_copy(s, d, local_sem.at[i]) for i, (s, d) in enumerate(moves)]
    for move in moves[:4]:
        move.start()

    barrier = pltpu.get_barrier_semaphore()
    mate_order = sorted(range(1, mates), key=lambda k: -min(k, mates - k))
    peer_order = sorted(range(1, planes), key=lambda k: -min(k, planes - k))
    near = [1, 2, planes - 2, planes - 1]
    partners = [mate(k) for k in mate_order] + [peer(k) for k in near]
    for partner in partners:
        pl.semaphore_signal(barrier, inc=1, device_id=partner, device_id_type=MESH)
    has_above, has_below = row < n_row - 1, row > 0
    has_after, has_before = device < total - 1, device > 0
    expected = len(partners)
    edges = [(has_above, above), (has_below, below), (has_after, after), (has_before, before)]
    for there, partner in edges:
        expected += jnp.where(there, 1, 0)

        @pl.when(there)
        def _(partner=partner):
            pl.semaphore_signal(barrier, inc=1, device_id=partner, device_id_type=MESH)

    for move in moves[4:]:
        move.start()

    square[...] = jnp.zeros_like(square)
    unused = lists.shape[0] - mates * capt
    lists[pl.ds(mates * capt, unused)] = jnp.full((unused, lists.shape[1]), -1, jnp.int32)
    moves[0].wait()
    moves[1].wait()
    square[pl.ds(0, classes), pl.ds(0, capt)] = tsrc[0]
    square[pl.ds(classes, classes), pl.ds(0, capt)] = ttgt[0]
    columns = square[...].T[:capt]
    mine[...] = columns
    lists[pl.ds(0, capt)] = columns

    def fine_counts(r, _):
        targets = onehot(b, ftgt[0, pl.ds(r, 1), :])
        sources = onehot(3 * b, fsrc[0, pl.ds(r, 1), :])
        cfine[r] = dot_nt(targets, sources).astype(BF)
        return 0

    moves[2].wait()
    moves[3].wait()
    lax.fori_loop(0, EARLY, fine_counts, 0, unroll=True)

    pl.semaphore_wait(barrier, expected)

    def remote(src, dst, send, recv, to):
        return pltpu.make_async_remote_copy(
            src_ref=src, dst_ref=dst, send_sem=send, recv_sem=recv, device_id=to, device_id_type=MESH
        )

    windows = [
        (own_top, twin.at[pl.ds(0, half)], above, has_above, has_below),
        (own_top, twin.at[pl.ds(2 * half, half)], below, has_below, has_above),
        (coarse_ref, cwin.at[pl.ds(0, cb)], after, has_after, has_before),
        (coarse_ref, cwin.at[pl.ds(2 * cb, cb)], before, has_before, has_after),
        (fine_ref, fwin.at[pl.ds(0, b)], after, has_after, has_before),
        (fine_ref, fwin.at[pl.ds(2 * b, b)], before, has_before, has_after),
    ]
    windows = [
        (remote(s, d, wsend.at[i], wrecv.at[i], to), d, sent, received)
        for i, (s, d, to, sent, received) in enumerate(windows)
    ]

    def start(window):
        pl.when(window[2])(window[0].start)

    def receive(window):
        pl.when(window[3])(window[0].wait_recv)

    posts = [
        remote(mine, lists.at[pl.ds(k * capt, capt)], lsend, lrecv, mate(k))
        for k in mate_order
    ]
    arrived = pl.ds(capt, (mates - 1) * capt)
    all_posts = remote(lists.at[arrived], lists.at[arrived], lsend, lrecv, mate(1))
    for copy in posts:
        copy.start()
    for window in windows:
        start(window)
    for k in (2, planes - 2):
        pl.semaphore_signal(learnt.at[0], inc=1, device_id=peer(k), device_id_type=MESH)
    for _, there, _, received in windows:

        @pl.when(jnp.logical_not(received))
        def _(there=there):
            there[...] = jnp.zeros(there.shape, BF)

    moves[4].wait()
    moves[5].wait()
    cpick[...] = jnp.full(cpick.shape, -1, jnp.int32)
    cpick[pl.ds(0, classes), pl.ds(0, capc)] = csrc[0] - (device - 1) * cb
    cpick[pl.ds(classes, classes), pl.ds(0, capc)] = ctgt[0]
    cwin[pl.ds(3 * cb, cwin.shape[0] - 3 * cb)] = jnp.zeros((cwin.shape[0] - 3 * cb, coeffs), BF)

    def coarse_counts(r, _):
        targets = onehot(cb, cpick[pl.ds(classes + r, 1), :])
        sources = onehot(cwin.shape[0], cpick[pl.ds(r, 1), :])
        ccoarse[pl.ds(pl.multiple_of(r * cb, cb), cb)] = dot_nt(targets, sources).astype(BF)
        return 0

    lax.fori_loop(0, classes, coarse_counts, 0, unroll=True)
    pl.semaphore_wait(learnt.at[0], 2)
    for k in (4, planes - 4):
        pl.semaphore_signal(learnt.at[1], inc=1, device_id=peer(k), device_id_type=MESH)
    lax.fori_loop(EARLY, MIDDLE, fine_counts, 0, unroll=True)

    all_posts.wait_recv()
    rows = lists[...].T[: 2 * classes]
    offset = rows[:classes] - (row - 1) * seg
    which = jnp.where(offset >= seg, 1, 0) + jnp.where(offset >= 2 * seg, 1, 0)
    inside = offset - which * seg - core * half
    inside = jnp.where((inside >= 0) & (inside < half), which * half + inside, -1)
    tpick[pl.ds(0, classes)] = inside
    tpick[pl.ds(classes, classes)] = rows[classes:] - x * quarter

    def class_columns(r):
        return pl.ds(r * coeffs, coeffs)

    moves[6].wait()
    receive(windows[0])
    receive(windows[1])
    moves[8].wait()

    def top_counts(r):
        targets = onehot(quarter, tpick[pl.ds(classes + r, 1), :])
        sources = onehot(3 * half, tpick[pl.ds(r, 1), :])
        return dot_nt(targets, sources).astype(BF)

    for first in range(0, classes, TOGETHER):
        group = range(first, first + TOGETHER)
        counts = jnp.concatenate([top_counts(r) for r in group], axis=0)
        hi, lo = split(dot(counts, twin[...]))
        for i, r in enumerate(group):
            atop[pl.ds(0, quarter), class_columns(r)] = hi[i * quarter : (i + 1) * quarter]
            atop[pl.ds(quarter, quarter), class_columns(r)] = lo[i * quarter : (i + 1) * quarter]
    part = dot(atop[...], ops[...].reshape(classes * coeffs, coeffs))
    part = part[:quarter] + part[quarter:]
    lanes = coeffs // 2
    left = part[:, :lanes].reshape(quarter // 8, 8, lanes)
    right = part[:, lanes:].reshape(quarter // 8, 8, lanes)
    low = lax.broadcasted_iota(jnp.int32, left.shape, 1) < 4
    even = jnp.where(low, left, pltpu.roll(right, 4, 1))
    odd = jnp.where(low, pltpu.roll(left, 4, 1), right)
    for i in range(quarter // 8):
        outbox[2 * i] = even[i]
        outbox[2 * i + 1] = odd[i]
    shares = [
        remote(outbox.at[lax.rem(j + k, planes)], inbox.at[k], rsend, rrecv, peer(k))
        for k in peer_order
    ]
    arrived = pl.ds(1, planes - 1)
    all_shares = remote(outbox.at[arrived], inbox.at[arrived], rsend, rrecv, peer(1))
    pl.semaphore_wait(learnt.at[1], 2)
    for copy in shares:
        copy.start()
    inbox[0] = outbox[j]

    lax.fori_loop(MIDDLE, classes, fine_counts, 0, unroll=True)

    for window in windows[2:4]:
        receive(window)
    moves[7].wait()

    hi, lo = split(dot(ccoarse[...], cwin[...]))
    for r in range(classes):
        acoarse[pl.ds(0, cb), class_columns(r)] = hi[r * cb : (r + 1) * cb]
        acoarse[pl.ds(cb, cb), class_columns(r)] = lo[r * cb : (r + 1) * cb]
    middle = dot(acoarse[...], ops[...].reshape(classes * coeffs, coeffs))
    middle = middle[:cb] + middle[cb:]

    for window in windows[4:]:
        receive(window)
    moves[9].wait()
    acc[...] = jnp.zeros_like(acc)

    def fine_rows(r, _):
        acc[...] += dot(dot(cfine[r], fwin[...]).astype(BF), ops[r])
        return 0

    lax.fori_loop(0, classes, fine_rows, 0, unroll=True)

    moves[10].wait()
    for window in windows:
        pl.when(window[2])(window[0].wait_send)
    all_posts.wait_send()
    all_shares.wait_send()
    all_shares.wait_recv()
    summed = inbox[0]
    for k in range(1, planes):
        summed += inbox[k]
    top = jnp.concatenate([summed[:4], summed[4:]], axis=1).astype(BF).astype(F32)
    coarse = children(top, l2l[...]) + middle
    coarse = coarse.astype(BF).astype(F32)
    parents = coarse.astype(BF)
    fine = jnp.stack([dot(parents, l2l[o]) for o in range(l2l.shape[0])], axis=1)
    out_ref[...] = fine.reshape(b, coeffs) + acc[...]


def solution(mesh):
    n_row, n_col = mesh.shape["row"], mesh.shape["col"]
    mates = XS * CORES
    planes = n_col // XS

    def per_device(*args):
        top, coarse, fine, m2l, l2l, tsrc, ttgt, csrc, ctgt, fsrc, ftgt = args
        classes, coeffs = m2l.shape[0], m2l.shape[1]
        seg, cb, b = top.shape[0], coarse.shape[0], fine.shape[0]
        quarter = seg // XS
        capt = tsrc.shape[2]
        pad = 128
        slots = -(-mates * capt // pad) * pad
        crows = -(-3 * cb // pad) * pad
        scratch = [
            pltpu.VMEM((3 * seg // CORES, coeffs), BF),
            pltpu.VMEM((crows, coeffs), BF),
            pltpu.VMEM((3 * b, coeffs), BF),
            pltpu.VMEM(m2l.shape, BF),
            pltpu.VMEM(l2l.shape, BF),
            *[pltpu.VMEM(a.shape, jnp.int32) for a in (tsrc, ttgt, csrc, ctgt, fsrc, ftgt)],
            pltpu.VMEM((pad, pad), jnp.int32),
            pltpu.VMEM((capt, pad), jnp.int32),
            pltpu.VMEM((slots, pad), jnp.int32),
            pltpu.VMEM((2 * classes, slots), jnp.int32),
            pltpu.VMEM((2 * classes, pad), jnp.int32),
            pltpu.VMEM((classes * cb, crows), BF),
            pltpu.VMEM((classes, b, 3 * b), BF),
            pltpu.VMEM((2 * quarter, classes * coeffs), BF),
            pltpu.VMEM((2 * cb, classes * coeffs), BF),
            pltpu.VMEM((b, coeffs), F32),
            pltpu.VMEM((planes, 8, coeffs // 2), F32),
            pltpu.VMEM((planes, 8, coeffs // 2), F32),
            pltpu.SemaphoreType.DMA((11,)),
            pltpu.SemaphoreType.DMA((6,)),
            pltpu.SemaphoreType.DMA((6,)),
            pltpu.SemaphoreType.DMA,
            pltpu.SemaphoreType.DMA,
            pltpu.SemaphoreType.DMA,
            pltpu.SemaphoreType.DMA,
            pltpu.SemaphoreType.REGULAR((2,)),
        ]
        return pl.pallas_call(
            functools.partial(kernel, n_row, n_col),
            out_shape=jax.ShapeDtypeStruct((b, coeffs), F32),
            in_specs=[pl.BlockSpec(memory_space=pltpu.HBM)] * len(args),
            out_specs=pl.BlockSpec(memory_space=pltpu.VMEM),
            scratch_shapes=scratch,
            compiler_params=pltpu.CompilerParams(
                collective_id=0, has_side_effects=True, vmem_limit_bytes=40 * 1024 * 1024
            ),
        )(*[pltpu.with_memory_space_constraint(a, pltpu.HBM) for a in args])

    both = P(("row", "col"), None)
    lists = P(("row", "col"), None, None)
    in_specs = (P("row", None), both, both, P(), P()) + (lists,) * 6
    return jax.shard_map(per_device, mesh=mesh, in_specs=in_specs, out_specs=both, check_vma=False)
```

```python
import functools

import jax
import jax.numpy as jnp
from jax import lax
from jax.experimental import pallas as pl
from jax.experimental.pallas import tpu as pltpu
from jax.sharding import PartitionSpec as P

CORES = 2
XS = 4
EARLY = 6
MIDDLE = 16
TOGETHER = 4
MESH = pl.DeviceIdType.MESH
BF = jnp.bfloat16
F32 = jnp.float32
F8 = jnp.float8_e4m3fn


def onehot(rows, picks):
    number = lax.broadcasted_iota(jnp.int32, (rows, picks.shape[1]), 0)
    return jnp.where(number == picks, 1.0, 0.0).astype(F8)


def dot(a, b):
    return jnp.dot(a, b, preferred_element_type=F32)


def dot_nt(a, b):
    return lax.dot_general(a, b, (((1,), (1,)), ((), ())), preferred_element_type=F32)


def split(a):
    hi = a.astype(BF)
    return hi, (a - hi.astype(F32)).astype(BF)


def children(parents, ops):
    n, c = parents.shape
    octants, depth, _ = ops.shape
    rep = jnp.broadcast_to(parents[:, None, :], (n, octants, c)).reshape(n * octants, c)
    which = lax.broadcasted_iota(jnp.int32, (n, octants, c), 1).reshape(n * octants, c)
    parts = [jnp.where(which == o, rep, 0.0).astype(BF) for o in range(octants)]
    return dot(jnp.concatenate(parts, axis=1), ops.reshape(octants * depth, c))


def kernel(
    n_row,
    n_col,
    top_ref,
    coarse_ref,
    fine_ref,
    m2l_ref,
    l2l_ref,
    tsrc_ref,
    ttgt_ref,
    csrc_ref,
    ctgt_ref,
    fsrc_ref,
    ftgt_ref,
    out_ref,
    twin,
    cwin,
    fwin,
    ops,
    l2l,
    tsrc,
    ttgt,
    csrc,
    ctgt,
    fsrc,
    ftgt,
    square,
    mine,
    lists,
    tpick,
    cpick,
    ccoarse,
    cfine,
    atop,
    acoarse,
    acc,
    outbox,
    inbox,
    local_sem,
    wsend,
    wrecv,
    lsend,
    lrecv,
    rsend,
    rrecv,
    learnt,
):
    classes, coeffs = m2l_ref.shape[0], m2l_ref.shape[1]
    seg = top_ref.shape[0]
    half = seg // CORES
    quarter = seg // XS
    cb, b = coarse_ref.shape[0], fine_ref.shape[0]
    capt = tsrc_ref.shape[2]
    capc = csrc_ref.shape[2]
    ys = n_col // (XS * CORES)
    mates = XS * CORES
    planes = ys * CORES

    row, col = lax.axis_index("row"), lax.axis_index("col")
    x, j = col // planes, lax.rem(col, planes)
    y, core = j // CORES, lax.rem(col, CORES)
    device = row * n_col + col
    total = n_row * n_col

    def place(index):
        return (index // n_col, lax.rem(index, n_col))

    after = place(lax.rem(device + 1, total))
    before = place(lax.rem(device + total - 1, total))
    above = (lax.rem(row + 1, n_row), col)
    below = (lax.rem(row + n_row - 1, n_row), col)

    def mate(k):
        m = lax.rem(x * CORES + core + k, mates)
        return (row, (m // CORES) * planes + y * CORES + lax.rem(m, CORES))

    def peer(k):
        return (row, x * planes + lax.rem(j + k, planes))

    own_top = top_ref.at[pl.ds(pl.multiple_of(core * half, half), half)]
    moves = [
        (tsrc_ref, tsrc),
        (ttgt_ref, ttgt),
        (fsrc_ref, fsrc),
        (ftgt_ref, ftgt),
        (csrc_ref, csrc),
        (ctgt_ref, ctgt),
        (own_top, twin.at[pl.ds(half, half)]),
        (coarse_ref, cwin.at[pl.ds(cb, cb)]),
        (m2l_ref, ops),
        (fine_ref, fwin.at[pl.ds(b, b)]),
        (l2l_ref, l2l),
    ]
    moves = [pltpu.make_async_copy(s, d, local_sem.at[i]) for i, (s, d) in enumerate(moves)]
    for move in moves[:4]:
        move.start()

    barrier = pltpu.get_barrier_semaphore()
    mate_order = sorted(range(1, mates), key=lambda k: -min(k, mates - k))
    peer_order = sorted(range(1, planes), key=lambda k: -min(k, planes - k))
    near = [1, 2, planes - 2, planes - 1]
    partners = [mate(k) for k in mate_order] + [peer(k) for k in near]
    for partner in partners:
        pl.semaphore_signal(barrier, inc=1, device_id=partner, device_id_type=MESH)
    has_above, has_below = row < n_row - 1, row > 0
    has_after, has_before = device < total - 1, device > 0
    expected = len(partners)
    edges = [(has_above, above), (has_below, below), (has_after, after), (has_before, before)]
    for there, partner in edges:
        expected += jnp.where(there, 1, 0)

        @pl.when(there)
        def _(partner=partner):
            pl.semaphore_signal(barrier, inc=1, device_id=partner, device_id_type=MESH)

    for move in moves[4:]:
        move.start()

    square[...] = jnp.zeros_like(square)
    unused = lists.shape[0] - mates * 8
    lists[pl.ds(mates * 8, unused)] = jnp.full((unused, lists.shape[1]), -1, jnp.int32)
    moves[0].wait()
    moves[1].wait()
    square[pl.ds(0, classes), pl.ds(0, capt)] = tsrc[0]
    square[pl.ds(classes, classes), pl.ds(0, capt)] = ttgt[0]
    columns = square[...].T
    packed = columns[:8]
    for g in range(1, capt // 8):
        packed += pltpu.roll(columns[8 * g : 8 * g + 8], g * 2 * classes, 1)
    mine[...] = packed
    lists[pl.ds(0, 8)] = packed

    def fine_counts(r, _):
        targets = onehot(b, ftgt[0, pl.ds(r, 1), :])
        sources = onehot(3 * b, fsrc[0, pl.ds(r, 1), :])
        cfine[r] = dot_nt(targets, sources).astype(BF)
        return 0

    moves[2].wait()
    moves[3].wait()
    lax.fori_loop(0, EARLY, fine_counts, 0, unroll=True)

    pl.semaphore_wait(barrier, expected)

    def remote(src, dst, send, recv, to):
        return pltpu.make_async_remote_copy(
            src_ref=src, dst_ref=dst, send_sem=send, recv_sem=recv, device_id=to, device_id_type=MESH
        )

    windows = [
        (own_top, twin.at[pl.ds(0, half)], above, has_above, has_below),
        (own_top, twin.at[pl.ds(2 * half, half)], below, has_below, has_above),
        (coarse_ref, cwin.at[pl.ds(0, cb)], after, has_after, has_before),
        (coarse_ref, cwin.at[pl.ds(2 * cb, cb)], before, has_before, has_after),
        (fine_ref, fwin.at[pl.ds(0, b)], after, has_after, has_before),
        (fine_ref, fwin.at[pl.ds(2 * b, b)], before, has_before, has_after),
    ]
    windows = [
        (remote(s, d, wsend.at[i], wrecv.at[i], to), d, sent, received)
        for i, (s, d, to, sent, received) in enumerate(windows)
    ]

    def start(window):
        pl.when(window[2])(window[0].start)

    def receive(window):
        pl.when(window[3])(window[0].wait_recv)

    posts = [
        remote(mine, lists.at[pl.ds(k * 8, 8)], lsend, lrecv, mate(k))
        for k in mate_order
    ]
    arrived = pl.ds(8, (mates - 1) * 8)
    all_posts = remote(lists.at[arrived], lists.at[arrived], lsend, lrecv, mate(1))
    for copy in posts:
        copy.start()
    for window in windows:
        start(window)
    for k in (2, planes - 2):
        pl.semaphore_signal(learnt.at[0], inc=1, device_id=peer(k), device_id_type=MESH)
    for _, there, _, received in windows:

        @pl.when(jnp.logical_not(received))
        def _(there=there):
            there[...] = jnp.zeros(there.shape, BF)

    moves[4].wait()
    moves[5].wait()
    cpick[...] = jnp.full(cpick.shape, -1, jnp.int32)
    cpick[pl.ds(0, classes), pl.ds(0, capc)] = csrc[0] - (device - 1) * cb
    cpick[pl.ds(classes, classes), pl.ds(0, capc)] = ctgt[0]
    cwin[pl.ds(3 * cb, cwin.shape[0] - 3 * cb)] = jnp.zeros((cwin.shape[0] - 3 * cb, coeffs), BF)

    def coarse_counts(r, _):
        targets = onehot(cb, cpick[pl.ds(classes + r, 1), :])
        sources = onehot(cwin.shape[0], cpick[pl.ds(r, 1), :])
        ccoarse[pl.ds(pl.multiple_of(r * cb, cb), cb)] = dot_nt(targets, sources).astype(BF)
        return 0

    lax.fori_loop(0, classes, coarse_counts, 0, unroll=True)
    pl.semaphore_wait(learnt.at[0], 2)
    for k in (4, planes - 4):
        pl.semaphore_signal(learnt.at[1], inc=1, device_id=peer(k), device_id_type=MESH)
    lax.fori_loop(EARLY, MIDDLE, fine_counts, 0, unroll=True)

    all_posts.wait_recv()
    turned = lists[...].T
    blocks = [turned[g * 2 * classes : (g + 1) * 2 * classes] for g in range(capt // 8)]
    lane = lax.broadcasted_iota(jnp.int32, blocks[0].shape, 1)
    pair = jnp.where(lane < 8 * mates, blocks[0], pltpu.roll(blocks[1], 8 * mates, 1))
    rows = jnp.concatenate([pair, blocks[2]], axis=1)
    offset = rows[:classes] - (row - 1) * seg
    which = jnp.where(offset >= seg, 1, 0) + jnp.where(offset >= 2 * seg, 1, 0)
    inside = offset - which * seg - core * half
    inside = jnp.where((inside >= 0) & (inside < half), which * half + inside, -1)
    tpick[pl.ds(0, classes)] = inside
    tpick[pl.ds(classes, classes)] = rows[classes:] - x * quarter

    def class_columns(r):
        return pl.ds(r * coeffs, coeffs)

    moves[6].wait()
    receive(windows[0])
    receive(windows[1])
    moves[8].wait()

    def top_counts(r):
        targets = onehot(quarter, tpick[pl.ds(classes + r, 1), :])
        sources = onehot(3 * half, tpick[pl.ds(r, 1), :])
        return dot_nt(targets, sources).astype(BF)

    for first in range(0, classes, TOGETHER):
        group = range(first, first + TOGETHER)
        counts = jnp.concatenate([top_counts(r) for r in group], axis=0)
        hi, lo = split(dot(counts, twin[...]))
        for i, r in enumerate(group):
            atop[pl.ds(0, quarter), class_columns(r)] = hi[i * quarter : (i + 1) * quarter]
            atop[pl.ds(quarter, quarter), class_columns(r)] = lo[i * quarter : (i + 1) * quarter]
    part = dot(atop[...], ops[...].reshape(classes * coeffs, coeffs))
    part = part[:quarter] + part[quarter:]
    lanes = coeffs // 2
    left = part[:, :lanes].reshape(quarter // 8, 8, lanes)
    right = part[:, lanes:].reshape(quarter // 8, 8, lanes)
    low = lax.broadcasted_iota(jnp.int32, left.shape, 1) < 4
    even = jnp.where(low, left, pltpu.roll(right, 4, 1))
    odd = jnp.where(low, pltpu.roll(left, 4, 1), right)
    for i in range(quarter // 8):
        outbox[2 * i] = even[i]
        outbox[2 * i + 1] = odd[i]
    shares = [
        remote(outbox.at[lax.rem(j + k, planes)], inbox.at[k], rsend, rrecv, peer(k))
        for k in peer_order
    ]
    arrived = pl.ds(1, planes - 1)
    all_shares = remote(outbox.at[arrived], inbox.at[arrived], rsend, rrecv, peer(1))
    pl.semaphore_wait(learnt.at[1], 2)
    for copy in shares:
        copy.start()
    inbox[0] = outbox[j]

    lax.fori_loop(MIDDLE, classes, fine_counts, 0, unroll=True)

    for window in windows[2:4]:
        receive(window)
    moves[7].wait()

    hi, lo = split(dot(ccoarse[...], cwin[...]))
    for r in range(classes):
        acoarse[pl.ds(0, cb), class_columns(r)] = hi[r * cb : (r + 1) * cb]
        acoarse[pl.ds(cb, cb), class_columns(r)] = lo[r * cb : (r + 1) * cb]
    middle = dot(acoarse[...], ops[...].reshape(classes * coeffs, coeffs))
    middle = middle[:cb] + middle[cb:]

    for window in windows[4:]:
        receive(window)
    moves[9].wait()
    acc[...] = jnp.zeros_like(acc)

    def fine_rows(r, _):
        acc[...] += dot(dot(cfine[r], fwin[...]).astype(BF), ops[r])
        return 0

    lax.fori_loop(0, classes, fine_rows, 0, unroll=True)

    moves[10].wait()
    for window in windows:
        pl.when(window[2])(window[0].wait_send)
    all_posts.wait_send()
    all_shares.wait_send()
    all_shares.wait_recv()
    summed = inbox[0]
    for k in range(1, planes):
        summed += inbox[k]
    top = jnp.concatenate([summed[:4], summed[4:]], axis=1).astype(BF).astype(F32)
    coarse = children(top, l2l[...]) + middle
    coarse = coarse.astype(BF).astype(F32)
    parents = coarse.astype(BF)
    fine = jnp.stack([dot(parents, l2l[o]) for o in range(l2l.shape[0])], axis=1)
    out_ref[...] = fine.reshape(b, coeffs) + acc[...]


def solution(mesh):
    n_row, n_col = mesh.shape["row"], mesh.shape["col"]
    mates = XS * CORES
    planes = n_col // XS

    def per_device(*args):
        top, coarse, fine, m2l, l2l, tsrc, ttgt, csrc, ctgt, fsrc, ftgt = args
        classes, coeffs = m2l.shape[0], m2l.shape[1]
        seg, cb, b = top.shape[0], coarse.shape[0], fine.shape[0]
        quarter = seg // XS
        capt = tsrc.shape[2]
        pad = 128
        slots = -(-mates * capt // pad) * pad
        crows = -(-3 * cb // pad) * pad
        scratch = [
            pltpu.VMEM((3 * seg // CORES, coeffs), BF),
            pltpu.VMEM((crows, coeffs), BF),
            pltpu.VMEM((3 * b, coeffs), BF),
            pltpu.VMEM(m2l.shape, BF),
            pltpu.VMEM(l2l.shape, BF),
            *[pltpu.VMEM(a.shape, jnp.int32) for a in (tsrc, ttgt, csrc, ctgt, fsrc, ftgt)],
            pltpu.VMEM((pad, pad), jnp.int32),
            pltpu.VMEM((8, pad), jnp.int32),
            pltpu.VMEM((pad, pad), jnp.int32),
            pltpu.VMEM((2 * classes, slots), jnp.int32),
            pltpu.VMEM((2 * classes, pad), jnp.int32),
            pltpu.VMEM((classes * cb, crows), BF),
            pltpu.VMEM((classes, b, 3 * b), BF),
            pltpu.VMEM((2 * quarter, classes * coeffs), BF),
            pltpu.VMEM((2 * cb, classes * coeffs), BF),
            pltpu.VMEM((b, coeffs), F32),
            pltpu.VMEM((planes, 8, coeffs // 2), F32),
            pltpu.VMEM((planes, 8, coeffs // 2), F32),
            pltpu.SemaphoreType.DMA((11,)),
            pltpu.SemaphoreType.DMA((6,)),
            pltpu.SemaphoreType.DMA((6,)),
            pltpu.SemaphoreType.DMA,
            pltpu.SemaphoreType.DMA,
            pltpu.SemaphoreType.DMA,
            pltpu.SemaphoreType.DMA,
            pltpu.SemaphoreType.REGULAR((2,)),
        ]
        return pl.pallas_call(
            functools.partial(kernel, n_row, n_col),
            out_shape=jax.ShapeDtypeStruct((b, coeffs), F32),
            in_specs=[pl.BlockSpec(memory_space=pltpu.HBM)] * len(args),
            out_specs=pl.BlockSpec(memory_space=pltpu.VMEM),
            scratch_shapes=scratch,
            compiler_params=pltpu.CompilerParams(
                collective_id=0, has_side_effects=True, vmem_limit_bytes=40 * 1024 * 1024
            ),
        )(*[pltpu.with_memory_space_constraint(a, pltpu.HBM) for a in args])

    both = P(("row", "col"), None)
    lists = P(("row", "col"), None, None)
    in_specs = (P("row", None), both, both, P(), P()) + (lists,) * 6
    return jax.shard_map(per_device, mesh=mesh, in_specs=in_specs, out_specs=both, check_vma=False)
```

```python
import functools

import jax
import jax.numpy as jnp
from jax import lax
from jax.experimental import pallas as pl
from jax.experimental.pallas import tpu as pltpu
from jax.sharding import PartitionSpec as P

CORES = 2
XS = 4
EARLY = 6
MIDDLE = 16
TOGETHER = 4
MESH = pl.DeviceIdType.MESH
BF = jnp.bfloat16
F32 = jnp.float32
F8 = jnp.float8_e4m3fn


def onehot(rows, picks):
    number = lax.broadcasted_iota(jnp.int32, (rows, picks.shape[1]), 0)
    return jnp.where(number == picks, 1.0, 0.0).astype(F8)


def dot(a, b):
    return jnp.dot(a, b, preferred_element_type=F32)


def dot_nt(a, b):
    return lax.dot_general(a, b, (((1,), (1,)), ((), ())), preferred_element_type=F32)


def split(a):
    hi = a.astype(BF)
    return hi, (a - hi.astype(F32)).astype(BF)


def children(parents, ops):
    n, c = parents.shape
    octants, depth, _ = ops.shape
    rep = jnp.broadcast_to(parents[:, None, :], (n, octants, c)).reshape(n * octants, c)
    which = lax.broadcasted_iota(jnp.int32, (n, octants, c), 1).reshape(n * octants, c)
    parts = [jnp.where(which == o, rep, 0.0).astype(BF) for o in range(octants)]
    return dot(jnp.concatenate(parts, axis=1), ops.reshape(octants * depth, c))


def kernel(
    n_row,
    n_col,
    top_ref,
    coarse_ref,
    fine_ref,
    m2l_ref,
    l2l_ref,
    tsrc_ref,
    ttgt_ref,
    csrc_ref,
    ctgt_ref,
    fsrc_ref,
    ftgt_ref,
    out_ref,
    twin,
    cwin,
    fwin,
    ops,
    l2l,
    tsrc,
    ttgt,
    csrc,
    ctgt,
    fsrc,
    ftgt,
    square,
    mine,
    lists,
    tpick,
    cpick,
    ccoarse,
    cfine,
    atop,
    acoarse,
    acc,
    outbox,
    inbox,
    local_sem,
    wsend,
    wrecv,
    lsend,
    lrecv,
    rsend,
    rrecv,
    learnt,
):
    classes, coeffs = m2l_ref.shape[0], m2l_ref.shape[1]
    seg = top_ref.shape[0]
    half = seg // CORES
    quarter = seg // XS
    cb, b = coarse_ref.shape[0], fine_ref.shape[0]
    capt = tsrc_ref.shape[2]
    capc = csrc_ref.shape[2]
    ys = n_col // (XS * CORES)
    mates = XS * CORES
    planes = ys * CORES

    row, col = lax.axis_index("row"), lax.axis_index("col")
    x, j = col // planes, lax.rem(col, planes)
    y, core = j // CORES, lax.rem(col, CORES)
    device = row * n_col + col
    total = n_row * n_col

    def place(index):
        return (index // n_col, lax.rem(index, n_col))

    after = place(lax.rem(device + 1, total))
    before = place(lax.rem(device + total - 1, total))
    above = (lax.rem(row + 1, n_row), col)
    below = (lax.rem(row + n_row - 1, n_row), col)

    def mate(k):
        m = lax.rem(x * CORES + core + k, mates)
        return (row, (m // CORES) * planes + y * CORES + lax.rem(m, CORES))

    def peer(k):
        return (row, x * planes + lax.rem(j + k, planes))

    own_top = top_ref.at[pl.ds(pl.multiple_of(core * half, half), half)]
    moves = [
        (tsrc_ref, tsrc),
        (ttgt_ref, ttgt),
        (fsrc_ref, fsrc),
        (ftgt_ref, ftgt),
        (csrc_ref, csrc),
        (ctgt_ref, ctgt),
        (own_top, twin.at[pl.ds(half, half)]),
        (coarse_ref, cwin.at[pl.ds(cb, cb)]),
        (m2l_ref, ops),
        (fine_ref, fwin.at[pl.ds(b, b)]),
        (l2l_ref, l2l),
    ]
    moves = [pltpu.make_async_copy(s, d, local_sem.at[i]) for i, (s, d) in enumerate(moves)]
    for move in moves[:4]:
        move.start()

    barrier = pltpu.get_barrier_semaphore()
    mate_order = sorted(range(1, mates), key=lambda k: -min(k, mates - k))
    peer_order = sorted(range(1, planes), key=lambda k: -min(k, planes - k))
    near = [1, 2, planes - 2, planes - 1]
    partners = [mate(k) for k in mate_order] + [peer(k) for k in near]
    for partner in partners:
        pl.semaphore_signal(barrier, inc=1, device_id=partner, device_id_type=MESH)
    has_above, has_below = row < n_row - 1, row > 0
    has_after, has_before = device < total - 1, device > 0
    expected = len(partners)
    edges = [(has_above, above), (has_below, below), (has_after, after), (has_before, before)]
    for there, partner in edges:
        expected += jnp.where(there, 1, 0)

        @pl.when(there)
        def _(partner=partner):
            pl.semaphore_signal(barrier, inc=1, device_id=partner, device_id_type=MESH)

    for move in moves[4:]:
        move.start()

    square[...] = jnp.zeros_like(square)
    unused = lists.shape[0] - mates * 8
    lists[pl.ds(mates * 8, unused)] = jnp.full((unused, lists.shape[1]), -1, jnp.int32)
    moves[0].wait()
    moves[1].wait()
    square[pl.ds(0, classes), pl.ds(0, capt)] = tsrc[0]
    square[pl.ds(classes, classes), pl.ds(0, capt)] = ttgt[0]
    columns = square[...].T
    packed = columns[:8]
    for g in range(1, capt // 8):
        packed += pltpu.roll(columns[8 * g : 8 * g + 8], g * 2 * classes, 1)
    mine[...] = packed
    lists[pl.ds(0, 8)] = packed

    def fine_counts(r, _):
        targets = onehot(b, ftgt[0, pl.ds(r, 1), :])
        sources = onehot(3 * b, fsrc[0, pl.ds(r, 1), :])
        cfine[r] = dot_nt(targets, sources).astype(BF)
        return 0

    moves[2].wait()
    moves[3].wait()
    lax.fori_loop(0, EARLY, fine_counts, 0, unroll=True)

    pl.semaphore_wait(barrier, expected)

    def remote(src, dst, send, recv, to):
        return pltpu.make_async_remote_copy(
            src_ref=src, dst_ref=dst, send_sem=send, recv_sem=recv, device_id=to, device_id_type=MESH
        )

    windows = [
        (own_top, twin.at[pl.ds(0, half)], above, has_above, has_below),
        (own_top, twin.at[pl.ds(2 * half, half)], below, has_below, has_above),
        (coarse_ref, cwin.at[pl.ds(0, cb)], after, has_after, has_before),
        (coarse_ref, cwin.at[pl.ds(2 * cb, cb)], before, has_before, has_after),
        (fine_ref, fwin.at[pl.ds(0, b)], after, has_after, has_before),
        (fine_ref, fwin.at[pl.ds(2 * b, b)], before, has_before, has_after),
    ]
    windows = [
        (remote(s, d, wsend.at[i], wrecv.at[i], to), d, sent, received)
        for i, (s, d, to, sent, received) in enumerate(windows)
    ]

    def start(window):
        pl.when(window[2])(window[0].start)

    def receive(window):
        pl.when(window[3])(window[0].wait_recv)

    posts = [
        remote(mine, lists.at[pl.ds(k * 8, 8)], lsend, lrecv, mate(k))
        for k in mate_order
    ]
    arrived = pl.ds(8, (mates - 1) * 8)
    all_posts = remote(lists.at[arrived], lists.at[arrived], lsend, lrecv, mate(1))
    for copy in posts:
        copy.start()
    for k in (2, planes - 2):
        pl.semaphore_signal(learnt.at[0], inc=1, device_id=peer(k), device_id_type=MESH)
    for window in windows:
        start(window)
    for _, there, _, received in windows:

        @pl.when(jnp.logical_not(received))
        def _(there=there):
            there[...] = jnp.zeros(there.shape, BF)

    moves[4].wait()
    moves[5].wait()
    cpick[...] = jnp.full(cpick.shape, -1, jnp.int32)
    cpick[pl.ds(0, classes), pl.ds(0, capc)] = csrc[0] - (device - 1) * cb
    cpick[pl.ds(classes, classes), pl.ds(0, capc)] = ctgt[0]
    cwin[pl.ds(3 * cb, cwin.shape[0] - 3 * cb)] = jnp.zeros((cwin.shape[0] - 3 * cb, coeffs), BF)

    def coarse_counts(r, _):
        targets = onehot(cb, cpick[pl.ds(classes + r, 1), :])
        sources = onehot(cwin.shape[0], cpick[pl.ds(r, 1), :])
        ccoarse[pl.ds(pl.multiple_of(r * cb, cb), cb)] = dot_nt(targets, sources).astype(BF)
        return 0

    lax.fori_loop(0, classes, coarse_counts, 0, unroll=True)
    lax.fori_loop(EARLY, MIDDLE, fine_counts, 0, unroll=True)
    pl.semaphore_wait(learnt.at[0], 2)
    for k in (4, planes - 4):
        pl.semaphore_signal(learnt.at[1], inc=1, device_id=peer(k), device_id_type=MESH)

    all_posts.wait_recv()
    turned = lists[...].T
    blocks = [turned[g * 2 * classes : (g + 1) * 2 * classes] for g in range(capt // 8)]
    lane = lax.broadcasted_iota(jnp.int32, blocks[0].shape, 1)
    pair = jnp.where(lane < 8 * mates, blocks[0], pltpu.roll(blocks[1], 8 * mates, 1))
    rows = jnp.concatenate([pair, blocks[2]], axis=1)
    offset = rows[:classes] - (row - 1) * seg
    which = jnp.where(offset >= seg, 1, 0) + jnp.where(offset >= 2 * seg, 1, 0)
    inside = offset - which * seg - core * half
    inside = jnp.where((inside >= 0) & (inside < half), which * half + inside, -1)
    tpick[pl.ds(0, classes)] = inside
    tpick[pl.ds(classes, classes)] = rows[classes:] - x * quarter

    def class_columns(r):
        return pl.ds(r * coeffs, coeffs)

    moves[6].wait()
    receive(windows[0])
    receive(windows[1])
    moves[8].wait()

    def top_counts(r):
        targets = onehot(quarter, tpick[pl.ds(classes + r, 1), :])
        sources = onehot(3 * half, tpick[pl.ds(r, 1), :])
        return dot_nt(targets, sources).astype(BF)

    for first in range(0, classes, TOGETHER):
        group = range(first, first + TOGETHER)
        counts = jnp.concatenate([top_counts(r) for r in group], axis=0)
        hi, lo = split(dot(counts, twin[...]))
        for i, r in enumerate(group):
            atop[pl.ds(0, quarter), class_columns(r)] = hi[i * quarter : (i + 1) * quarter]
            atop[pl.ds(quarter, quarter), class_columns(r)] = lo[i * quarter : (i + 1) * quarter]
    part = dot(atop[...], ops[...].reshape(classes * coeffs, coeffs))
    part = part[:quarter] + part[quarter:]
    lanes = coeffs // 2
    left = part[:, :lanes].reshape(quarter // 8, 8, lanes)
    right = part[:, lanes:].reshape(quarter // 8, 8, lanes)
    low = lax.broadcasted_iota(jnp.int32, left.shape, 1) < 4
    even = jnp.where(low, left, pltpu.roll(right, 4, 1))
    odd = jnp.where(low, pltpu.roll(left, 4, 1), right)
    for i in range(quarter // 8):
        outbox[2 * i] = even[i]
        outbox[2 * i + 1] = odd[i]
    shares = [
        remote(outbox.at[lax.rem(j + k, planes)], inbox.at[k], rsend, rrecv, peer(k))
        for k in peer_order
    ]
    arrived = pl.ds(1, planes - 1)
    all_shares = remote(outbox.at[arrived], inbox.at[arrived], rsend, rrecv, peer(1))
    pl.semaphore_wait(learnt.at[1], 2)
    for copy in shares:
        copy.start()
    inbox[0] = outbox[j]

    lax.fori_loop(MIDDLE, classes, fine_counts, 0, unroll=True)

    for window in windows[2:4]:
        receive(window)
    moves[7].wait()

    hi, lo = split(dot(ccoarse[...], cwin[...]))
    for r in range(classes):
        acoarse[pl.ds(0, cb), class_columns(r)] = hi[r * cb : (r + 1) * cb]
        acoarse[pl.ds(cb, cb), class_columns(r)] = lo[r * cb : (r + 1) * cb]
    middle = dot(acoarse[...], ops[...].reshape(classes * coeffs, coeffs))
    middle = middle[:cb] + middle[cb:]

    for window in windows[4:]:
        receive(window)
    moves[9].wait()
    acc[...] = jnp.zeros_like(acc)

    def fine_rows(r, _):
        acc[...] += dot(dot(cfine[r], fwin[...]).astype(BF), ops[r])
        return 0

    lax.fori_loop(0, classes, fine_rows, 0, unroll=True)

    moves[10].wait()
    for window in windows:
        pl.when(window[2])(window[0].wait_send)
    all_posts.wait_send()
    all_shares.wait_send()
    all_shares.wait_recv()
    summed = inbox[0]
    for k in range(1, planes):
        summed += inbox[k]
    top = jnp.concatenate([summed[:4], summed[4:]], axis=1).astype(BF).astype(F32)
    coarse = children(top, l2l[...]) + middle
    coarse = coarse.astype(BF).astype(F32)
    parents = coarse.astype(BF)
    fine = jnp.stack([dot(parents, l2l[o]) for o in range(l2l.shape[0])], axis=1)
    out_ref[...] = fine.reshape(b, coeffs) + acc[...]


def solution(mesh):
    n_row, n_col = mesh.shape["row"], mesh.shape["col"]
    mates = XS * CORES
    planes = n_col // XS

    def per_device(*args):
        top, coarse, fine, m2l, l2l, tsrc, ttgt, csrc, ctgt, fsrc, ftgt = args
        classes, coeffs = m2l.shape[0], m2l.shape[1]
        seg, cb, b = top.shape[0], coarse.shape[0], fine.shape[0]
        quarter = seg // XS
        capt = tsrc.shape[2]
        pad = 128
        slots = -(-mates * capt // pad) * pad
        crows = -(-3 * cb // pad) * pad
        scratch = [
            pltpu.VMEM((3 * seg // CORES, coeffs), BF),
            pltpu.VMEM((crows, coeffs), BF),
            pltpu.VMEM((3 * b, coeffs), BF),
            pltpu.VMEM(m2l.shape, BF),
            pltpu.VMEM(l2l.shape, BF),
            *[pltpu.VMEM(a.shape, jnp.int32) for a in (tsrc, ttgt, csrc, ctgt, fsrc, ftgt)],
            pltpu.VMEM((pad, pad), jnp.int32),
            pltpu.VMEM((8, pad), jnp.int32),
            pltpu.VMEM((pad, pad), jnp.int32),
            pltpu.VMEM((2 * classes, slots), jnp.int32),
            pltpu.VMEM((2 * classes, pad), jnp.int32),
            pltpu.VMEM((classes * cb, crows), BF),
            pltpu.VMEM((classes, b, 3 * b), BF),
            pltpu.VMEM((2 * quarter, classes * coeffs), BF),
            pltpu.VMEM((2 * cb, classes * coeffs), BF),
            pltpu.VMEM((b, coeffs), F32),
            pltpu.VMEM((planes, 8, coeffs // 2), F32),
            pltpu.VMEM((planes, 8, coeffs // 2), F32),
            pltpu.SemaphoreType.DMA((11,)),
            pltpu.SemaphoreType.DMA((6,)),
            pltpu.SemaphoreType.DMA((6,)),
            pltpu.SemaphoreType.DMA,
            pltpu.SemaphoreType.DMA,
            pltpu.SemaphoreType.DMA,
            pltpu.SemaphoreType.DMA,
            pltpu.SemaphoreType.REGULAR((2,)),
        ]
        return pl.pallas_call(
            functools.partial(kernel, n_row, n_col),
            out_shape=jax.ShapeDtypeStruct((b, coeffs), F32),
            in_specs=[pl.BlockSpec(memory_space=pltpu.HBM)] * len(args),
            out_specs=pl.BlockSpec(memory_space=pltpu.VMEM),
            scratch_shapes=scratch,
            compiler_params=pltpu.CompilerParams(
                collective_id=0, has_side_effects=True, vmem_limit_bytes=40 * 1024 * 1024
            ),
        )(*[pltpu.with_memory_space_constraint(a, pltpu.HBM) for a in args])

    both = P(("row", "col"), None)
    lists = P(("row", "col"), None, None)
    in_specs = (P("row", None), both, both, P(), P()) + (lists,) * 6
    return jax.shard_map(per_device, mesh=mesh, in_specs=in_specs, out_specs=both, check_vma=False)
```

```python
import functools

import jax
import jax.numpy as jnp
from jax import lax
from jax.experimental import pallas as pl
from jax.experimental.pallas import tpu as pltpu
from jax.sharding import PartitionSpec as P

CORES = 2
XS = 4
EARLY = 4
MIDDLE = 13
TOGETHER = 4
MESH = pl.DeviceIdType.MESH
BF = jnp.bfloat16
F32 = jnp.float32
F8 = jnp.float8_e4m3fn


def onehot(rows, picks):
    number = lax.broadcasted_iota(jnp.int32, (rows, picks.shape[1]), 0)
    return jnp.where(number == picks, 1.0, 0.0).astype(F8)


def dot(a, b):
    return jnp.dot(a, b, preferred_element_type=F32)


def dot_nt(a, b):
    return lax.dot_general(a, b, (((1,), (1,)), ((), ())), preferred_element_type=F32)


def split(a):
    hi = a.astype(BF)
    return hi, (a - hi.astype(F32)).astype(BF)


def children(parents, ops):
    n, c = parents.shape
    octants, depth, _ = ops.shape
    rep = jnp.broadcast_to(parents[:, None, :], (n, octants, c)).reshape(n * octants, c)
    which = lax.broadcasted_iota(jnp.int32, (n, octants, c), 1).reshape(n * octants, c)
    parts = [jnp.where(which == o, rep, 0.0).astype(BF) for o in range(octants)]
    return dot(jnp.concatenate(parts, axis=1), ops.reshape(octants * depth, c))


def kernel(
    n_row,
    n_col,
    top_ref,
    coarse_ref,
    fine_ref,
    m2l_ref,
    l2l_ref,
    tsrc_ref,
    ttgt_ref,
    csrc_ref,
    ctgt_ref,
    fsrc_ref,
    ftgt_ref,
    out_ref,
    twin,
    cwin,
    fwin,
    ops,
    l2l,
    tsrc,
    ttgt,
    csrc,
    ctgt,
    fsrc,
    ftgt,
    square,
    mine,
    lists,
    tpick,
    cpick,
    ccoarse,
    cfine,
    atop,
    acoarse,
    acc,
    outbox,
    inbox,
    local_sem,
    wsend,
    wrecv,
    lsend,
    lrecv,
    rsend,
    rrecv,
    learnt,
):
    classes, coeffs = m2l_ref.shape[0], m2l_ref.shape[1]
    seg = top_ref.shape[0]
    half = seg // CORES
    quarter = seg // XS
    cb, b = coarse_ref.shape[0], fine_ref.shape[0]
    capt = tsrc_ref.shape[2]
    capc = csrc_ref.shape[2]
    ys = n_col // (XS * CORES)
    mates = XS * CORES
    planes = ys * CORES

    row, col = lax.axis_index("row"), lax.axis_index("col")
    x, j = col // planes, lax.rem(col, planes)
    y, core = j // CORES, lax.rem(col, CORES)
    device = row * n_col + col
    total = n_row * n_col

    def place(index):
        return (index // n_col, lax.rem(index, n_col))

    after = place(lax.rem(device + 1, total))
    before = place(lax.rem(device + total - 1, total))
    above = (lax.rem(row + 1, n_row), col)
    below = (lax.rem(row + n_row - 1, n_row), col)

    def mate(k):
        m = lax.rem(x * CORES + core + k, mates)
        return (row, (m // CORES) * planes + y * CORES + lax.rem(m, CORES))

    def peer(k):
        return (row, x * planes + lax.rem(j + k, planes))

    own_top = top_ref.at[pl.ds(pl.multiple_of(core * half, half), half)]
    moves = [
        (tsrc_ref, tsrc),
        (ttgt_ref, ttgt),
        (fsrc_ref, fsrc),
        (ftgt_ref, ftgt),
        (csrc_ref, csrc),
        (ctgt_ref, ctgt),
        (own_top, twin.at[pl.ds(half, half)]),
        (coarse_ref, cwin.at[pl.ds(cb, cb)]),
        (m2l_ref, ops),
        (fine_ref, fwin.at[pl.ds(b, b)]),
        (l2l_ref, l2l),
    ]
    moves = [pltpu.make_async_copy(s, d, local_sem.at[i]) for i, (s, d) in enumerate(moves)]
    for move in moves[:4]:
        move.start()

    barrier = pltpu.get_barrier_semaphore()
    mate_order = sorted(range(1, mates), key=lambda k: -min(k, mates - k))
    peer_order = sorted(range(1, planes), key=lambda k: -min(k, planes - k))
    near = [1, 2, planes - 2, planes - 1]
    partners = [mate(k) for k in mate_order] + [peer(k) for k in near]
    for partner in partners:
        pl.semaphore_signal(barrier, inc=1, device_id=partner, device_id_type=MESH)
    has_above, has_below = row < n_row - 1, row > 0
    has_after, has_before = device < total - 1, device > 0
    expected = len(partners)
    edges = [(has_above, above), (has_below, below), (has_after, after), (has_before, before)]
    for there, partner in edges:
        expected += jnp.where(there, 1, 0)

        @pl.when(there)
        def _(partner=partner):
            pl.semaphore_signal(barrier, inc=1, device_id=partner, device_id_type=MESH)

    for move in moves[4:]:
        move.start()

    square[...] = jnp.zeros_like(square)
    unused = lists.shape[0] - mates * 8
    lists[pl.ds(mates * 8, unused)] = jnp.full((unused, lists.shape[1]), -1, jnp.int32)
    moves[0].wait()
    moves[1].wait()
    square[pl.ds(0, classes), pl.ds(0, capt)] = tsrc[0]
    square[pl.ds(classes, classes), pl.ds(0, capt)] = ttgt[0]
    columns = square[...].T
    packed = columns[:8]
    for g in range(1, capt // 8):
        packed += pltpu.roll(columns[8 * g : 8 * g + 8], g * 2 * classes, 1)
    mine[...] = packed
    lists[pl.ds(0, 8)] = packed

    def fine_counts(r, _):
        targets = onehot(b, ftgt[0, pl.ds(r, 1), :])
        sources = onehot(3 * b, fsrc[0, pl.ds(r, 1), :])
        cfine[r] = dot_nt(targets, sources).astype(BF)
        return 0

    moves[2].wait()
    moves[3].wait()
    lax.fori_loop(0, EARLY, fine_counts, 0, unroll=True)

    pl.semaphore_wait(barrier, expected)

    def remote(src, dst, send, recv, to):
        return pltpu.make_async_remote_copy(
            src_ref=src, dst_ref=dst, send_sem=send, recv_sem=recv, device_id=to, device_id_type=MESH
        )

    windows = [
        (own_top, twin.at[pl.ds(0, half)], above, has_above, has_below),
        (own_top, twin.at[pl.ds(2 * half, half)], below, has_below, has_above),
        (coarse_ref, cwin.at[pl.ds(0, cb)], after, has_after, has_before),
        (coarse_ref, cwin.at[pl.ds(2 * cb, cb)], before, has_before, has_after),
        (fine_ref, fwin.at[pl.ds(0, b)], after, has_after, has_before),
        (fine_ref, fwin.at[pl.ds(2 * b, b)], before, has_before, has_after),
    ]
    windows = [
        (remote(s, d, wsend.at[i], wrecv.at[i], to), d, sent, received)
        for i, (s, d, to, sent, received) in enumerate(windows)
    ]

    def start(window):
        pl.when(window[2])(window[0].start)

    def receive(window):
        pl.when(window[3])(window[0].wait_recv)

    posts = [
        remote(mine, lists.at[pl.ds(k * 8, 8)], lsend, lrecv, mate(k))
        for k in mate_order
    ]
    arrived = pl.ds(8, (mates - 1) * 8)
    all_posts = remote(lists.at[arrived], lists.at[arrived], lsend, lrecv, mate(1))
    for copy in posts:
        copy.start()
    for k in (2, planes - 2):
        pl.semaphore_signal(learnt.at[0], inc=1, device_id=peer(k), device_id_type=MESH)
    for window in windows:
        start(window)
    for _, there, _, received in windows:

        @pl.when(jnp.logical_not(received))
        def _(there=there):
            there[...] = jnp.zeros(there.shape, BF)

    moves[4].wait()
    moves[5].wait()
    cpick[...] = jnp.full(cpick.shape, -1, jnp.int32)
    cpick[pl.ds(0, classes), pl.ds(0, capc)] = csrc[0] - (device - 1) * cb
    cpick[pl.ds(classes, classes), pl.ds(0, capc)] = ctgt[0]
    cwin[pl.ds(3 * cb, cwin.shape[0] - 3 * cb)] = jnp.zeros((cwin.shape[0] - 3 * cb, coeffs), BF)

    def coarse_counts(r, _):
        targets = onehot(cb, cpick[pl.ds(classes + r, 1), :])
        sources = onehot(cwin.shape[0], cpick[pl.ds(r, 1), :])
        ccoarse[pl.ds(pl.multiple_of(r * cb, cb), cb)] = dot_nt(targets, sources).astype(BF)
        return 0

    lax.fori_loop(0, classes, coarse_counts, 0, unroll=True)
    lax.fori_loop(EARLY, MIDDLE, fine_counts, 0, unroll=True)
    pl.semaphore_wait(learnt.at[0], 2)
    for k in (4, planes - 4):
        pl.semaphore_signal(learnt.at[1], inc=1, device_id=peer(k), device_id_type=MESH)

    all_posts.wait_recv()
    turned = lists[...].T
    blocks = [turned[g * 2 * classes : (g + 1) * 2 * classes] for g in range(capt // 8)]
    lane = lax.broadcasted_iota(jnp.int32, blocks[0].shape, 1)
    pair = jnp.where(lane < 8 * mates, blocks[0], pltpu.roll(blocks[1], 8 * mates, 1))
    rows = jnp.concatenate([pair, blocks[2]], axis=1)
    offset = rows[:classes] - (row - 1) * seg
    which = jnp.where(offset >= seg, 1, 0) + jnp.where(offset >= 2 * seg, 1, 0)
    inside = offset - which * seg - core * half
    inside = jnp.where((inside >= 0) & (inside < half), which * half + inside, -1)
    tpick[pl.ds(0, classes)] = inside
    tpick[pl.ds(classes, classes)] = rows[classes:] - x * quarter

    def class_columns(r):
        return pl.ds(r * coeffs, coeffs)

    moves[6].wait()
    receive(windows[0])
    receive(windows[1])
    moves[8].wait()

    def top_counts(r):
        targets = onehot(quarter, tpick[pl.ds(classes + r, 1), :])
        sources = onehot(3 * half, tpick[pl.ds(r, 1), :])
        return dot_nt(targets, sources).astype(BF)

    for first in range(0, classes, TOGETHER):
        group = range(first, first + TOGETHER)
        counts = jnp.concatenate([top_counts(r) for r in group], axis=0)
        hi, lo = split(dot(counts, twin[...]))
        for i, r in enumerate(group):
            atop[pl.ds(0, quarter), class_columns(r)] = hi[i * quarter : (i + 1) * quarter]
            atop[pl.ds(quarter, quarter), class_columns(r)] = lo[i * quarter : (i + 1) * quarter]
    part = dot(atop[...], ops[...].reshape(classes * coeffs, coeffs))
    part = part[:quarter] + part[quarter:]
    lanes = coeffs // 2
    left = part[:, :lanes].reshape(quarter // 8, 8, lanes)
    right = part[:, lanes:].reshape(quarter // 8, 8, lanes)
    low = lax.broadcasted_iota(jnp.int32, left.shape, 1) < 4
    even = jnp.where(low, left, pltpu.roll(right, 4, 1))
    odd = jnp.where(low, pltpu.roll(left, 4, 1), right)
    for i in range(quarter // 8):
        outbox[2 * i] = even[i]
        outbox[2 * i + 1] = odd[i]
    shares = [
        remote(outbox.at[lax.rem(j + k, planes)], inbox.at[k], rsend, rrecv, peer(k))
        for k in peer_order
    ]
    arrived = pl.ds(1, planes - 1)
    all_shares = remote(outbox.at[arrived], inbox.at[arrived], rsend, rrecv, peer(1))
    pl.semaphore_wait(learnt.at[1], 2)
    for copy in shares:
        copy.start()
    inbox[0] = outbox[j]

    lax.fori_loop(MIDDLE, classes, fine_counts, 0, unroll=True)

    for window in windows[2:4]:
        receive(window)
    moves[7].wait()

    hi, lo = split(dot(ccoarse[...], cwin[...]))
    for r in range(classes):
        acoarse[pl.ds(0, cb), class_columns(r)] = hi[r * cb : (r + 1) * cb]
        acoarse[pl.ds(cb, cb), class_columns(r)] = lo[r * cb : (r + 1) * cb]
    middle = dot(acoarse[...], ops[...].reshape(classes * coeffs, coeffs))
    middle = middle[:cb] + middle[cb:]

    for window in windows[4:]:
        receive(window)
    moves[9].wait()
    acc[...] = jnp.zeros_like(acc)

    def fine_rows(r, _):
        acc[...] += dot(dot(cfine[r], fwin[...]).astype(BF), ops[r])
        return 0

    lax.fori_loop(0, classes, fine_rows, 0, unroll=True)

    moves[10].wait()
    for window in windows:
        pl.when(window[2])(window[0].wait_send)
    all_posts.wait_send()
    all_shares.wait_send()
    all_shares.wait_recv()
    summed = inbox[0]
    for k in range(1, planes):
        summed += inbox[k]
    top = jnp.concatenate([summed[:4], summed[4:]], axis=1).astype(BF).astype(F32)
    coarse = children(top, l2l[...]) + middle
    coarse = coarse.astype(BF).astype(F32)
    parents = coarse.astype(BF)
    fine = jnp.stack([dot(parents, l2l[o]) for o in range(l2l.shape[0])], axis=1)
    out_ref[...] = fine.reshape(b, coeffs) + acc[...]


def solution(mesh):
    n_row, n_col = mesh.shape["row"], mesh.shape["col"]
    mates = XS * CORES
    planes = n_col // XS

    def per_device(*args):
        top, coarse, fine, m2l, l2l, tsrc, ttgt, csrc, ctgt, fsrc, ftgt = args
        classes, coeffs = m2l.shape[0], m2l.shape[1]
        seg, cb, b = top.shape[0], coarse.shape[0], fine.shape[0]
        quarter = seg // XS
        capt = tsrc.shape[2]
        pad = 128
        slots = -(-mates * capt // pad) * pad
        crows = -(-3 * cb // pad) * pad
        scratch = [
            pltpu.VMEM((3 * seg // CORES, coeffs), BF),
            pltpu.VMEM((crows, coeffs), BF),
            pltpu.VMEM((3 * b, coeffs), BF),
            pltpu.VMEM(m2l.shape, BF),
            pltpu.VMEM(l2l.shape, BF),
            *[pltpu.VMEM(a.shape, jnp.int32) for a in (tsrc, ttgt, csrc, ctgt, fsrc, ftgt)],
            pltpu.VMEM((pad, pad), jnp.int32),
            pltpu.VMEM((8, pad), jnp.int32),
            pltpu.VMEM((pad, pad), jnp.int32),
            pltpu.VMEM((2 * classes, slots), jnp.int32),
            pltpu.VMEM((2 * classes, pad), jnp.int32),
            pltpu.VMEM((classes * cb, crows), BF),
            pltpu.VMEM((classes, b, 3 * b), BF),
            pltpu.VMEM((2 * quarter, classes * coeffs), BF),
            pltpu.VMEM((2 * cb, classes * coeffs), BF),
            pltpu.VMEM((b, coeffs), F32),
            pltpu.VMEM((planes, 8, coeffs // 2), F32),
            pltpu.VMEM((planes, 8, coeffs // 2), F32),
            pltpu.SemaphoreType.DMA((11,)),
            pltpu.SemaphoreType.DMA((6,)),
            pltpu.SemaphoreType.DMA((6,)),
            pltpu.SemaphoreType.DMA,
            pltpu.SemaphoreType.DMA,
            pltpu.SemaphoreType.DMA,
            pltpu.SemaphoreType.DMA,
            pltpu.SemaphoreType.REGULAR((2,)),
        ]
        return pl.pallas_call(
            functools.partial(kernel, n_row, n_col),
            out_shape=jax.ShapeDtypeStruct((b, coeffs), F32),
            in_specs=[pl.BlockSpec(memory_space=pltpu.HBM)] * len(args),
            out_specs=pl.BlockSpec(memory_space=pltpu.VMEM),
            scratch_shapes=scratch,
            compiler_params=pltpu.CompilerParams(
                collective_id=0, has_side_effects=True, vmem_limit_bytes=40 * 1024 * 1024
            ),
        )(*[pltpu.with_memory_space_constraint(a, pltpu.HBM) for a in args])

    both = P(("row", "col"), None)
    lists = P(("row", "col"), None, None)
    in_specs = (P("row", None), both, both, P(), P()) + (lists,) * 6
    return jax.shard_map(per_device, mesh=mesh, in_specs=in_specs, out_specs=both, check_vma=False)
```
